32 devices in a mesh: frame: 8 (over z, y), band: 4 (over x, core).
Axes of the slice: x: 2, y: 2, z: 4, core: 2. Of those that a mesh axis runs over, the one named last changes fastest.
Arguments:
- latents: bfloat16 [8, 64, 32, 640], P('frame', 'band'), may hold values from -90 to 90, as said below
- conv_weight: bfloat16 [3, 3, 640, 640], replicated, may hold values from -0.078125 to 0.078125
- conv_bias: bfloat16 [640], replicated, may hold values from -3 to 3
- w_query: bfloat16 [640, 640], replicated, may hold values from -0.25 to 0.25
- w_keyval: bfloat16 [640, 1280], replicated, may hold values from -0.25 to 0.25
- w_out: bfloat16 [640, 640], replicated, may hold values from -0.25 to 0.25
Outputs:
- result: bfloat16 [8, 64, 32, 640], P('frame', 'band')
The draws below stay inside these ranges and needn't reach their ends.
Inputs may be any that keep to these rules, and one draw needn't show every extreme that they name: `latents`: latent features; some frames may be far larger in magnitude than others.
All inputs are finite; a program needn't handle non-finite values.
Results may differ from the reference program's by a relative error of at most 0.023.
Values may be sent and summed in bfloat16 or wider, within the bound.
No kernel may reach another device: no remote copies, remote signals or barrier semaphores. Data moves between devices by JAX's collectives and lax.ppermute only.
A program may use at most 128 MiB of HBM per device.

```python
import jax
import jax.numpy as jnp
from jax import lax

CHANNELS = 640
HEAD_DIM = 64
WIDTH = 32
HEADS = 10
FRAMES = 8
HEIGHT = 64


def draw_latents(key, part):
    values = jax.random.normal(jax.random.fold_in(key, 11), (FRAMES, HEIGHT, WIDTH, CHANNELS), jnp.float32)
    values = jnp.clip(values, -5.0, 5.0)
    return values.astype(jnp.bfloat16)


def bell_draw(own_key, dims, width, limit, held_as=jnp.bfloat16):
    entries = width * jax.random.normal(own_key, dims, jnp.float32)
    return jnp.clip(entries, min=-limit, max=limit).astype(held_as)


def setup_inputs(seed: int = 0) -> dict:
    splits = jax.random.split(jax.random.key(seed), 7)
    return {
        "latents": draw_latents(jax.random.fold_in(splits[6], 71), 0),
        "conv_weight": bell_draw(splits[1], (3, 3, CHANNELS, CHANNELS), (9 * CHANNELS) ** -0.5, 0.078125),
        "conv_bias": bell_draw(splits[2], (CHANNELS,), 0.5, 3.0),
        "w_query": bell_draw(splits[3], (CHANNELS, CHANNELS), CHANNELS ** -0.5, 0.25),
        "w_keyval": bell_draw(splits[4], (CHANNELS, 2 * CHANNELS), CHANNELS ** -0.5, 0.25),
        "w_out": bell_draw(splits[5], (CHANNELS, CHANNELS), CHANNELS ** -0.5, 0.25),
    }


def conv_frame(frame, conv_weight, conv_bias):
    activated = jax.nn.silu(frame.astype(jnp.float32)).astype(jnp.bfloat16)
    padded = jnp.pad(activated, ((1, 1), (1, 1), (0, 0)))
    row_count, col_count, channels = frame.shape
    tokens = row_count * col_count
    summed = jnp.zeros((tokens, channels), jnp.float32)
    for row_shift in range(3):
        for col_shift in range(3):
            window = padded[row_shift:row_shift + row_count, col_shift:col_shift + col_count].reshape(tokens, channels)
            summed = summed + jnp.dot(window, conv_weight[row_shift, col_shift], preferred_element_type=jnp.float32)
    hidden = frame.reshape(tokens, channels).astype(jnp.float32) + summed + conv_bias.astype(jnp.float32)
    return hidden.astype(jnp.bfloat16)


def attend_all(queries, keys, values):
    query_count = queries.shape[0]
    key_count = keys.shape[0]
    query_heads = queries.reshape(query_count, HEADS, HEAD_DIM).astype(jnp.float32)
    key_heads = keys.reshape(key_count, HEADS, HEAD_DIM).astype(jnp.float32)
    value_heads = values.reshape(key_count, HEADS, HEAD_DIM).astype(jnp.float32)
    scores = jnp.einsum("qhd,khd->hqk", query_heads, key_heads) * (HEAD_DIM ** -0.5)
    row_best = jnp.max(scores, axis=2, keepdims=True)
    probability = jnp.exp(scores - row_best)
    total = jnp.sum(probability, axis=2)
    rounded = probability.astype(jnp.bfloat16).astype(jnp.float32)
    mixed = jnp.einsum("hqk,khd->qhd", rounded, value_heads)
    mixed = mixed / jnp.transpose(total)[:, :, None]
    return mixed.reshape(query_count, CHANNELS).astype(jnp.bfloat16)


def reference(latents, conv_weight, conv_bias, w_query, w_keyval, w_out):
    hidden = lax.map(lambda frame: conv_frame(frame, conv_weight, conv_bias), latents)
    keyval = jnp.dot(hidden[0], w_keyval, preferred_element_type=jnp.float32).astype(jnp.bfloat16)
    keys = keyval[:, :CHANNELS]
    values = keyval[:, CHANNELS:]

    def one_frame(frame_tokens):
        queries = jnp.dot(frame_tokens, w_query, preferred_element_type=jnp.float32).astype(jnp.bfloat16)
        mixed = attend_all(queries, keys, values)
        output = frame_tokens.astype(jnp.float32) + jnp.dot(mixed, w_out, preferred_element_type=jnp.float32)
        return output.astype(jnp.bfloat16)

    result = lax.map(one_frame, hidden)
    return result.reshape(FRAMES, HEIGHT, WIDTH, CHANNELS)
```

```python
import functools

import jax
import jax.numpy as jnp
from jax import lax
from jax.experimental import pallas as pl
from jax.experimental.pallas import tpu as pltpu
from jax.sharding import PartitionSpec as P

HEAD_DIM = 64
PAIR = 2 * HEAD_DIM
VMEM_BYTES = 56 * 2**20


def conv_kernel(
    width, x_ref, low_ref, high_ref, weight_hbm, bias_ref, query_hbm, hidden_ref, queries_ref,
    weight, w_query, taps, sems,
):
    tokens, channels = x_ref.shape
    order = (1, 0, 2)
    copies = [
        pltpu.make_async_copy(weight_hbm.at[shift], weight.at[shift], sems.at[shift])
        for shift in range(3)
    ]
    for shift in order:
        copies[shift].start()
    query_copy = pltpu.make_async_copy(query_hbm, w_query, sems.at[3])
    query_copy.start()

    padded = tokens + 2 * width
    raw = jnp.concatenate([low_ref[...], x_ref[...], high_ref[...]], axis=0).astype(jnp.float32)
    active = raw * jax.nn.sigmoid(raw)
    column = lax.rem(lax.broadcasted_iota(jnp.int32, (padded, 1), 0), width)
    before = jnp.where(column == 0, 0.0, pltpu.roll(active, 1, 0))
    after = jnp.where(column == width - 1, 0.0, pltpu.roll(active, padded - 1, 0))
    taps[:, :channels] = before.astype(jnp.bfloat16)
    taps[:, channels : 2 * channels] = active.astype(jnp.bfloat16)
    taps[:, 2 * channels :] = after.astype(jnp.bfloat16)

    total = x_ref[...].astype(jnp.float32) + bias_ref[...].astype(jnp.float32)
    for shift in order:
        copies[shift].wait()
        total = total + jnp.dot(
            taps[shift * width : shift * width + tokens, :],
            weight[shift],
            preferred_element_type=jnp.float32,
        )
    hidden = total.astype(jnp.bfloat16)
    hidden_ref[...] = hidden
    query_copy.wait()
    queries = jnp.dot(hidden, w_query[...], preferred_element_type=jnp.float32)
    queries_ref[...] = queries.astype(jnp.bfloat16)


def convolve(x, low, high, conv_weight, conv_bias, w_query, width):
    tokens, channels = x.shape
    in_vmem = pl.BlockSpec(memory_space=pltpu.VMEM)
    in_place = pl.BlockSpec(memory_space=pl.ANY)
    token_array = jax.ShapeDtypeStruct((tokens, channels), jnp.bfloat16)
    return pl.pallas_call(
        functools.partial(conv_kernel, width),
        out_shape=(token_array, token_array),
        in_specs=[in_vmem, in_vmem, in_vmem, in_place, in_vmem, in_place],
        out_specs=(in_vmem, in_vmem),
        scratch_shapes=[
            pltpu.VMEM((3, 3 * channels, channels), jnp.bfloat16),
            pltpu.VMEM((channels, channels), jnp.bfloat16),
            pltpu.VMEM((tokens + 2 * width, 3 * channels), jnp.bfloat16),
            pltpu.SemaphoreType.DMA((4,)),
        ],
        compiler_params=pltpu.CompilerParams(vmem_limit_bytes=VMEM_BYTES),
        cost_estimate=pl.CostEstimate(
            flops=20 * tokens * channels * channels,
            bytes_accessed=20 * channels * channels + 6 * tokens * channels,
            transcendentals=0,
        ),
        name="convolve",
    )(
        x, low, high,
        conv_weight.reshape(3, 3 * channels, channels), conv_bias.reshape(1, channels), w_query,
    )


def attend_kernel(piece_count, *refs):
    queries_ref, hidden_ref, keyval_hbm, out_hbm = refs[:4]
    pieces = refs[4 : 4 + piece_count]
    result_ref, w_keyval, w_out, keys, values, mixed, sems = refs[4 + piece_count :]
    tokens, channels = queries_ref.shape
    keyval_copy = pltpu.make_async_copy(keyval_hbm, w_keyval, sems.at[0])
    out_copy = pltpu.make_async_copy(out_hbm, w_out, sems.at[1])
    keyval_copy.start()
    out_copy.start()
    keyval_copy.wait()
    start = 0
    for piece in pieces:
        count = piece.shape[0]
        keyval = jnp.dot(piece[...], w_keyval[...], preferred_element_type=jnp.float32)
        keyval = keyval.astype(jnp.bfloat16)
        keys[start : start + count, :] = keyval[:, :channels]
        values[start : start + count, :] = keyval[:, channels:]
        start += count
    lane = lax.broadcasted_iota(jnp.int32, (tokens, PAIR), 1)
    ones = jnp.ones((start, PAIR), jnp.bfloat16)
    for first in range(0, channels, PAIR):
        lanes = slice(first, first + PAIR)
        both = queries_ref[:, lanes] * HEAD_DIM ** (-0.5)
        nothing = jnp.zeros_like(both)
        split = jnp.concatenate(
            [jnp.where(lane < HEAD_DIM, both, nothing), jnp.where(lane < HEAD_DIM, nothing, both)], axis=0
        )
        scores = lax.dot_general(
            split, keys[:, lanes], (((1,), (1,)), ((), ())), preferred_element_type=jnp.float32
        )
        probability = jnp.exp(scores - jnp.max(scores, axis=1, keepdims=True)).astype(jnp.bfloat16)
        weighted = jnp.dot(
            probability,
            jnp.concatenate([values[:, lanes], ones], axis=1),
            preferred_element_type=jnp.float32,
        )
        heads = weighted[:, :PAIR] / weighted[:, PAIR:]
        mixed[:, lanes] = jnp.where(lane < HEAD_DIM, heads[:tokens], heads[tokens:]).astype(jnp.bfloat16)
    out_copy.wait()
    result = hidden_ref[...].astype(jnp.float32) + jnp.dot(
        mixed[...], w_out[...], preferred_element_type=jnp.float32
    )
    result_ref[...] = result.astype(jnp.bfloat16)


def attend(queries, hidden, w_keyval, w_out, pieces):
    tokens, channels = queries.shape
    key_count = sum(piece.shape[0] for piece in pieces)
    in_vmem = pl.BlockSpec(memory_space=pltpu.VMEM)
    in_place = pl.BlockSpec(memory_space=pl.ANY)
    return pl.pallas_call(
        functools.partial(attend_kernel, len(pieces)),
        out_shape=jax.ShapeDtypeStruct((tokens, channels), jnp.bfloat16),
        in_specs=[in_vmem, in_vmem, in_place, in_place] + [in_vmem] * len(pieces),
        out_specs=in_vmem,
        scratch_shapes=[
            pltpu.VMEM(w_keyval.shape, jnp.bfloat16),
            pltpu.VMEM(w_out.shape, jnp.bfloat16),
            pltpu.VMEM((key_count, channels), jnp.bfloat16),
            pltpu.VMEM((key_count, channels), jnp.bfloat16),
            pltpu.VMEM((tokens, channels), jnp.bfloat16),
            pltpu.SemaphoreType.DMA((2,)),
        ],
        compiler_params=pltpu.CompilerParams(vmem_limit_bytes=VMEM_BYTES),
        cost_estimate=pl.CostEstimate(
            flops=4 * tokens * key_count * channels,
            bytes_accessed=2 * channels * (key_count + 3 * tokens),
            transcendentals=tokens * key_count * channels // HEAD_DIM,
        ),
        name="attend",
    )(queries, hidden, w_keyval, w_out, *pieces)


def from_edges(block, axis):
    count = lax.axis_size(axis)
    forward = [(i, i + 1) for i in range(count - 1)]
    backward = [(target, source) for source, target in forward]
    low = lax.ppermute(block[:, -1], axis, forward)
    high = lax.ppermute(block[:, 0], axis, backward)
    return low, high


def swap(value, axis, distance):
    pairs = [(i, i ^ distance) for i in range(lax.axis_size(axis))]
    return lax.ppermute(value, axis, pairs)


def spread(hidden):
    frame_count, band_count = lax.axis_size("frame"), lax.axis_size("band")
    frame = lax.axis_index("frame")
    half = hidden.shape[0] // 2
    other = lax.ppermute(hidden[half:], "frame", [(0, 1)])
    mine = jnp.where(frame == 0, hidden[:half], other)
    reach = frame_count // 2
    while reach > 1:
        reach //= 2
        starts = range(0, frame_count, 4 * reach)
        pairs = [(i + y, i + 2 * reach + y) for i in starts for y in range(2)]
        arrived = lax.ppermute(mine, "frame", pairs)
        mine = jnp.where(lax.rem(frame // 2, 2 * reach) == reach, arrived, mine)
    beside = swap(mine, "frame", 1)
    pieces = [mine, beside]
    across = band_count
    while across > 2:
        across //= 2
        pieces = pieces + [swap(piece, "band", across) for piece in pieces]
    return pieces + [swap(piece, "band", 1) for piece in pieces]


def per_device(latents, conv_weight, conv_bias, w_query, w_keyval, w_out):
    frames, row_count, col_count, channels = latents.shape
    low, high = from_edges(latents, "band")
    hidden, queries = [], []
    for frame in range(frames):
        block = latents[frame].reshape(row_count * col_count, channels)
        parts = convolve(block, low[frame], high[frame], conv_weight, conv_bias, w_query, col_count)
        hidden.append(parts[0])
        queries.append(parts[1])
    pieces = spread(hidden[0])
    results = [
        attend(queries[frame], hidden[frame], w_keyval, w_out, pieces) for frame in range(frames)
    ]
    return jnp.stack(results).reshape(latents.shape)


def solution(mesh):
    return jax.shard_map(
        per_device,
        mesh=mesh,
        in_specs=(P("frame", "band", None, None), P(), P(), P(), P(), P()),
        out_specs=P("frame", "band", None, None),
        check_vma=False,
    )
```

```python
import functools

import jax
import jax.numpy as jnp
from jax import lax
from jax.experimental import pallas as pl
from jax.experimental.pallas import tpu as pltpu
from jax.sharding import PartitionSpec as P

HEAD_DIM = 64
PAIR = 2 * HEAD_DIM
VMEM_BYTES = 40 * 2**20
IN_VMEM = pl.BlockSpec(memory_space=pltpu.VMEM)
IN_PLACE = pl.BlockSpec(memory_space=pl.ANY)


def conv_kernel(width, spans, splits, x_hbm, low_ref, high_ref, weight_hbm, bias_ref, *refs):
    outs = refs[: len(splits)]
    rows, weight, taps, sems = refs[len(splits) :]
    tokens, channels = x_hbm.shape
    last_row = tokens // width
    order = (1, 0, 2)

    loads, edges, starts, place = [], [], [], 0
    for first, count in spans:
        begin, end = max(first - 1, 0), min(first + count + 1, last_row)
        starts.append(place)
        if first == 0:
            edges.append((low_ref, place))
            place += 1
        loads.append((begin, end - begin, place))
        place += end - begin
        if first + count == last_row:
            edges.append((high_ref, place))
            place += 1
    copies = [
        pltpu.make_async_copy(
            x_hbm.at[pl.ds(begin * width, count * width)],
            rows.at[pl.ds(spot * width, count * width)],
            sems.at[3 + i],
        )
        for i, (begin, count, spot) in enumerate(loads)
    ]
    for copy in copies:
        copy.start()
    weight_copies = [
        pltpu.make_async_copy(weight_hbm.at[shift], weight.at[shift], sems.at[shift])
        for shift in range(3)
    ]
    for shift in order:
        weight_copies[shift].start()
    for edge_ref, spot in edges:
        rows[spot * width : (spot + 1) * width, :] = edge_ref[...]
    for copy in copies:
        copy.wait()

    padded = place * width
    raw = rows[...].astype(jnp.float32)
    active = raw * jax.nn.sigmoid(raw)
    column = lax.rem(lax.broadcasted_iota(jnp.int32, (padded, 1), 0), width)
    before = jnp.where(column == 0, 0.0, pltpu.roll(active, 1, 0))
    after = jnp.where(column == width - 1, 0.0, pltpu.roll(active, padded - 1, 0))
    taps[:, :channels] = before.astype(jnp.bfloat16)
    taps[:, channels : 2 * channels] = active.astype(jnp.bfloat16)
    taps[:, 2 * channels :] = after.astype(jnp.bfloat16)

    def rows_at(ref, shift):
        parts = [
            ref[(start + shift) * width : (start + shift + count) * width, :]
            for start, (_, count) in zip(starts, spans)
        ]
        return parts[0] if len(parts) == 1 else jnp.concatenate(parts, axis=0)

    total = rows_at(rows, 1).astype(jnp.float32) + bias_ref[...].astype(jnp.float32)[None, :]
    for shift in order:
        weight_copies[shift].wait()
        total = total + jnp.dot(
            rows_at(taps, shift), weight[shift], preferred_element_type=jnp.float32
        )
    place = 0
    for out, size in zip(outs, splits):
        out[...] = total[place : place + size].astype(jnp.bfloat16)
        place += size


def convolve(x, low, high, conv_weight, conv_bias, width, spans, splits, name):
    tokens, channels = x.shape
    made = sum(splits)
    gathered = made + 2 * width * len(spans)
    return pl.pallas_call(
        functools.partial(conv_kernel, width, spans, splits),
        out_shape=tuple(jax.ShapeDtypeStruct((size, channels), jnp.bfloat16) for size in splits),
        in_specs=[IN_PLACE, IN_VMEM, IN_VMEM, IN_PLACE, IN_VMEM],
        out_specs=(IN_VMEM,) * len(splits),
        scratch_shapes=[
            pltpu.VMEM((gathered, channels), jnp.bfloat16),
            pltpu.VMEM((3, 3 * channels, channels), jnp.bfloat16),
            pltpu.VMEM((gathered, 3 * channels), jnp.bfloat16),
            pltpu.SemaphoreType.DMA((3 + len(spans),)),
        ],
        compiler_params=pltpu.CompilerParams(vmem_limit_bytes=VMEM_BYTES),
        cost_estimate=pl.CostEstimate(
            flops=18 * made * channels * channels,
            bytes_accessed=18 * channels * channels + 4 * made * channels,
            transcendentals=0,
        ),
        name=name,
    )(x, low, high, conv_weight, conv_bias)


def query_kernel(layout, *refs):
    count = len(layout)
    pieces, (w_query, hidden_ref, queries_ref) = refs[:count], refs[count:]
    for piece, spots in zip(pieces, layout):
        taken = 0
        for start, size in spots:
            hidden_ref[start : start + size, :] = piece[taken : taken + size, :]
            taken += size
    queries = jnp.dot(hidden_ref[...], w_query[...], preferred_element_type=jnp.float32)
    queries_ref[...] = queries.astype(jnp.bfloat16)


def ask(pieces, layout, w_query):
    tokens, channels = sum(piece.shape[0] for piece in pieces), w_query.shape[0]
    whole = jax.ShapeDtypeStruct((tokens, channels), jnp.bfloat16)
    return pl.pallas_call(
        functools.partial(query_kernel, layout),
        out_shape=(whole, whole),
        in_specs=[IN_VMEM] * (len(pieces) + 1),
        out_specs=(IN_VMEM, IN_VMEM),
        compiler_params=pltpu.CompilerParams(vmem_limit_bytes=16 * 2**20),
        cost_estimate=pl.CostEstimate(
            flops=2 * tokens * channels * channels,
            bytes_accessed=2 * channels * channels + 6 * tokens * channels,
            transcendentals=0,
        ),
        name="ask",
    )(*pieces, w_query)


def attend_kernel(piece_count, first, last, queries_ref, keyval_hbm, *refs):
    refs = list(refs)
    pieces = [refs.pop(0) for _ in range(piece_count)]
    old = None if first else [refs.pop(0) for _ in range(3)]
    ending = [refs.pop(0) for _ in range(2)] if last else None
    new = [refs.pop(0) for _ in range(1 if last else 3)]
    w_keyval, w_out, keys, values, mixed, sems = refs
    tokens, channels = queries_ref.shape
    keyval_copy = pltpu.make_async_copy(keyval_hbm, w_keyval, sems.at[0])
    keyval_copy.start()
    if last:
        out_copy = pltpu.make_async_copy(ending[1], w_out, sems.at[1])
        out_copy.start()
    keyval_copy.wait()
    key_count = 0
    for piece in pieces:
        spot = slice(key_count, key_count + piece.shape[0])
        keyval = jnp.dot(piece[...], w_keyval[...], preferred_element_type=jnp.float32)
        keyval = keyval.astype(jnp.bfloat16)
        keys[spot, :] = keyval[:, :channels]
        values[spot, :] = keyval[:, channels:]
        key_count = spot.stop
    is_low = lax.broadcasted_iota(jnp.int32, (tokens, PAIR), 1) < HEAD_DIM
    ones = jnp.ones((key_count, PAIR), jnp.bfloat16)
    for start in range(0, channels, PAIR):
        lanes = slice(start, start + PAIR)
        both = queries_ref[:, lanes] * HEAD_DIM ** (-0.5)
        nothing = jnp.zeros_like(both)
        split = jnp.concatenate(
            [jnp.where(is_low, both, nothing), jnp.where(is_low, nothing, both)], axis=0
        )
        scores = lax.dot_general(
            split, keys[:, lanes], (((1,), (1,)), ((), ())), preferred_element_type=jnp.float32
        )
        best = jnp.max(scores, axis=1, keepdims=True)
        best_pair = jnp.where(is_low, best[:tokens], best[tokens:])
        if not first:
            best_pair = jnp.maximum(best_pair, old[2][:, lanes])
            best = jnp.concatenate(
                [best_pair[:, :1], best_pair[:, HEAD_DIM : HEAD_DIM + 1]], axis=0
            )
        probability = jnp.exp(scores - best).astype(jnp.bfloat16)
        product = jnp.dot(
            probability,
            jnp.concatenate([values[:, lanes], ones], axis=1),
            preferred_element_type=jnp.float32,
        )
        weighted = jnp.where(is_low, product[:tokens, :PAIR], product[tokens:, :PAIR])
        total = jnp.where(is_low, product[:tokens, PAIR:], product[tokens:, PAIR:])
        if not first:
            fading = jnp.exp(old[2][:, lanes] - best_pair)
            weighted = weighted + old[0][:, lanes] * fading
            total = total + old[1][:, lanes] * fading
        if last:
            mixed[:, lanes] = (weighted / total).astype(jnp.bfloat16)
        else:
            new[0][:, lanes] = weighted
            new[1][:, lanes] = total
            new[2][:, lanes] = best_pair
    if last:
        out_copy.wait()
        result = ending[0][...].astype(jnp.float32) + jnp.dot(
            mixed[...], w_out[...], preferred_element_type=jnp.float32
        )
        new[0][...] = result.astype(jnp.bfloat16)


def attend(queries, w_keyval, pieces, state, ending, name):
    tokens, channels = queries.shape
    key_count = sum(piece.shape[0] for piece in pieces)
    first, last = state is None, ending is not None
    part = jax.ShapeDtypeStruct((tokens, channels), jnp.float32)
    whole = jax.ShapeDtypeStruct((tokens, channels), jnp.bfloat16)
    args = [queries, w_keyval, *pieces, *(() if first else state), *(ending if last else ())]
    in_specs = [IN_VMEM] * len(args)
    in_specs[1] = IN_PLACE
    if last:
        in_specs[-1] = IN_PLACE
    return pl.pallas_call(
        functools.partial(attend_kernel, len(pieces), first, last),
        out_shape=whole if last else (part,) * 3,
        in_specs=in_specs,
        out_specs=IN_VMEM if last else (IN_VMEM,) * 3,
        scratch_shapes=[
            pltpu.VMEM(w_keyval.shape, jnp.bfloat16),
            pltpu.VMEM((channels, channels), jnp.bfloat16),
            pltpu.VMEM((key_count, channels), jnp.bfloat16),
            pltpu.VMEM((key_count, channels), jnp.bfloat16),
            pltpu.VMEM((tokens, channels), jnp.bfloat16),
            pltpu.SemaphoreType.DMA((2,)),
        ],
        compiler_params=pltpu.CompilerParams(vmem_limit_bytes=VMEM_BYTES),
        cost_estimate=pl.CostEstimate(
            flops=4 * tokens * key_count * channels,
            bytes_accessed=2 * channels * (key_count + 3 * tokens),
            transcendentals=tokens * key_count * channels // HEAD_DIM,
        ),
        name=name,
    )(*args)


def from_edges(block, axis):
    count = lax.axis_size(axis)
    forward = [(i, i + 1) for i in range(count - 1)]
    backward = [(target, source) for source, target in forward]
    low = lax.ppermute(block[:, -1], axis, forward)
    high = lax.ppermute(block[:, 0], axis, backward)
    return low, high


def cast(even, odd):
    frame_count = lax.axis_size("frame")
    frame = lax.axis_index("frame")
    held = jnp.zeros_like(even)
    reach = frame_count // 2
    while reach > 1:
        arrived = [
            lax.ppermute(even, "frame", [(0, reach)]),
            lax.ppermute(odd, "frame", [(0, reach + 1)]),
        ]
        relays = [
            (i + y, i + reach + y) for i in range(2 * reach, frame_count, 2 * reach) for y in range(2)
        ]
        if relays:
            arrived.append(lax.ppermute(held, "frame", relays))
            arrived.append(held)
        held = functools.reduce(jnp.add, arrived)
        reach //= 2
    held = held + lax.ppermute(odd, "frame", [(0, 1)])
    return jnp.where(frame == 0, even, held)


def swap(value, axes, distances):
    sizes = [lax.axis_size(axis) for axis in axes]
    pairs = []
    for i in range(sizes[0]):
        for j in range(sizes[1]):
            other = (i ^ distances[0]) * sizes[1] + (j ^ distances[1])
            pairs.append((i * sizes[1] + j, other))
    return lax.ppermute(value, axes, pairs)


def per_device(latents, conv_weight, conv_bias, w_query, w_keyval, w_out):
    frames, row_count, width, channels = latents.shape
    tokens = row_count * width
    half, quarter = row_count // 2, tokens // 4
    taps_weight = conv_weight.reshape(3, 3 * channels, channels)
    no_edge = jnp.zeros((width, channels), latents.dtype)
    low, high = from_edges(latents, "band")
    inner = ((1, half),)
    outer = ((0, 1), (half + 1, row_count - half - 1))
    seam = (half + 1) * width
    layout = (
        ((width, quarter),),
        ((width + quarter, quarter),),
        ((0, width), (seam, quarter - width)),
        ((seam + quarter - width, quarter),),
    )
    parts = []
    for frame in range(frames):
        block = latents[frame].reshape(tokens, channels)
        parts.append(
            convolve(
                block, no_edge, no_edge, taps_weight, conv_bias, width, inner, (quarter,) * 2, "inner"
            )
            + convolve(
                block, low[frame], high[frame], taps_weight, conv_bias, width, outer, (quarter,) * 2,
                "outer",
            )
        )
    asked = [ask(part, layout, w_query) for part in parts]

    axes = ("frame", "band")
    chunks = []
    for even, odd in ((parts[0][0], parts[0][1]), (parts[0][2], parts[0][3])):
        mine = cast(even, odd)
        chunks.append(
            [mine, swap(mine, axes, (1, 0)), swap(mine, axes, (0, 2)), swap(mine, axes, (1, 2))]
        )
    chunks = [[(piece, swap(piece, axes, (0, 1))) for piece in chunk] for chunk in chunks]
    groups = [
        [*chunks[0][0], *chunks[0][1], *chunks[0][2]],
        [*chunks[0][3], *chunks[1][0]],
        [*chunks[1][1], *chunks[1][2], *chunks[1][3]],
    ]
    results = []
    for hidden, queries in asked:
        state = None
        for i, group in enumerate(groups):
            ending = (hidden, w_out) if i == len(groups) - 1 else None
            state = attend(queries, w_keyval, group, state, ending, f"attend{i}")
        results.append(state)
    return jnp.stack(results).reshape(latents.shape)


def solution(mesh):
    return jax.shard_map(
        per_device,
        mesh=mesh,
        in_specs=(P("frame", "band", None, None), P(), P(), P(), P(), P()),
        out_specs=P("frame", "band", None, None),
        check_vma=False,
    )
```

```python
import functools

import jax
import jax.numpy as jnp
from jax import lax
from jax.experimental import pallas as pl
from jax.experimental.pallas import tpu as pltpu
from jax.sharding import PartitionSpec as P

HEAD_DIM = 64
PAIR = 2 * HEAD_DIM
VMEM_BYTES = 40 * 2**20
CONV_VMEM_BYTES = 44 * 2**20
IN_VMEM = pl.BlockSpec(memory_space=pltpu.VMEM)
IN_PLACE = pl.BlockSpec(memory_space=pl.ANY)
IN_HBM = pl.BlockSpec(memory_space=pltpu.HBM)
SHIFTS = (1, 0, 2)
QUICK = pl.CostEstimate(flops=1, bytes_accessed=1, transcendentals=0)


def conv_span(width, spans, x_hbm, low_ref, high_ref, weight, bias_ref, rows, taps, sems, before_use):
    tokens, channels = x_hbm.shape
    last_row = tokens // width
    loads, edges, starts, place = [], [], [], 0
    for first, count in spans:
        begin, end = max(first - 1, 0), min(first + count + 1, last_row)
        starts.append(place)
        if first == 0:
            edges.append((low_ref, place))
            place += 1
        loads.append((begin, end - begin, place))
        place += end - begin
        if first + count == last_row:
            edges.append((high_ref, place))
            place += 1
    copies = [
        pltpu.make_async_copy(
            x_hbm.at[pl.ds(begin * width, count * width)],
            rows.at[pl.ds(spot * width, count * width)],
            sems.at[i],
        )
        for i, (begin, count, spot) in enumerate(loads)
    ]
    for copy in copies:
        copy.start()
    waits = before_use()
    for edge_ref, spot in edges:
        rows[spot * width : (spot + 1) * width, :] = edge_ref[...]
    for copy in copies:
        copy.wait()

    padded = place * width
    raw = rows[:padded, :].astype(jnp.float32)
    active = raw * jax.nn.sigmoid(raw)
    column = lax.rem(lax.broadcasted_iota(jnp.int32, (padded, 1), 0), width)
    before = jnp.where(column == 0, 0.0, pltpu.roll(active, 1, 0))
    after = jnp.where(column == width - 1, 0.0, pltpu.roll(active, padded - 1, 0))
    taps[:padded, :channels] = before.astype(jnp.bfloat16)
    taps[:padded, channels : 2 * channels] = active.astype(jnp.bfloat16)
    taps[:padded, 2 * channels :] = after.astype(jnp.bfloat16)

    def rows_at(ref, shift):
        parts = [
            ref[(start + shift) * width : (start + shift + count) * width, :]
            for start, (_, count) in zip(starts, spans)
        ]
        return parts[0] if len(parts) == 1 else jnp.concatenate(parts, axis=0)

    total = rows_at(rows, 1).astype(jnp.float32) + bias_ref[...].astype(jnp.float32)[None, :]
    for shift in SHIFTS:
        if waits:
            waits[shift].wait()
        total = total + jnp.dot(
            rows_at(taps, shift), weight[shift], preferred_element_type=jnp.float32
        )
    return total.astype(jnp.bfloat16)


def inner_kernel(width, spans, x_hbm, weight_hbm, bias_ref, out_ref, weight, rows, taps, sems):
    copies = [
        pltpu.make_async_copy(weight_hbm.at[shift], weight.at[shift], sems.at[shift])
        for shift in range(3)
    ]

    def fetch():
        for shift in SHIFTS:
            copies[shift].start()
        return copies

    @pl.when(lax.axis_index("frame") == 0)
    def _():
        out_ref[...] = conv_span(
            width, spans, x_hbm, None, None, weight, bias_ref, rows, taps, sems.at[pl.ds(3, len(spans))], fetch
        )

    @pl.when(lax.axis_index("frame") != 0)
    def _():
        for copy in fetch():
            copy.wait()


def outer_kernel(
    width, inner, outer, redo, x_hbm, low_ref, high_ref, weight, bias_ref, first_ref, out_ref, inner_ref,
    rows, taps, sems,
):
    def compute(spans):
        return conv_span(
            width, spans, x_hbm, low_ref, high_ref, weight, bias_ref, rows, taps,
            sems.at[pl.ds(0, len(spans))], lambda: None,
        )

    out_ref[...] = compute(outer)
    if redo:
        inner_ref[...] = compute(inner)
    else:
        @pl.when(lax.axis_index("frame") != 0)
        def _():
            inner_ref[...] = compute(inner)

        @pl.when(lax.axis_index("frame") == 0)
        def _():
            inner_ref[...] = first_ref[...]


def scratch_for(span_rows, width, channels, copies):
    return [
        pltpu.VMEM((span_rows * width, channels), jnp.bfloat16),
        pltpu.VMEM((span_rows * width, 3 * channels), jnp.bfloat16),
        pltpu.SemaphoreType.DMA((copies,)),
    ]


def convolve_inner(x, taps_weight, bias, width, inner):
    channels = x.shape[1]
    made = sum(count for _, count in inner)
    return pl.pallas_call(
        functools.partial(inner_kernel, width, inner),
        out_shape=(
            jax.ShapeDtypeStruct((made * width, channels), jnp.bfloat16),
            jax.ShapeDtypeStruct(taps_weight.shape, jnp.bfloat16),
        ),
        in_specs=[IN_HBM, IN_HBM, IN_VMEM],
        out_specs=(IN_VMEM, IN_VMEM),
        scratch_shapes=scratch_for(made + 2, width, channels, 3 + len(inner)),
        compiler_params=pltpu.CompilerParams(vmem_limit_bytes=CONV_VMEM_BYTES),
        cost_estimate=QUICK,
        name="inner",
    )(x, taps_weight, bias)


def convolve_outer(x, low, high, taps_weight, bias, first, width, inner, outer, redo):
    channels = x.shape[1]
    made = [sum(count for _, count in spans) for spans in (outer, inner)]
    padded = max(made[0] + 2 * len(outer), made[1] + 2 * len(inner))
    return pl.pallas_call(
        functools.partial(outer_kernel, width, inner, outer, redo),
        out_shape=tuple(jax.ShapeDtypeStruct((n * width, channels), jnp.bfloat16) for n in made),
        in_specs=[IN_HBM, IN_VMEM, IN_VMEM, IN_VMEM, IN_VMEM, IN_VMEM],
        out_specs=(IN_VMEM, IN_VMEM),
        scratch_shapes=scratch_for(padded, width, channels, max(len(inner), len(outer))),
        compiler_params=pltpu.CompilerParams(vmem_limit_bytes=CONV_VMEM_BYTES),
        cost_estimate=QUICK,
        name="outer",
    )(x, low, high, taps_weight, bias, first)


def query_kernel(layout, *refs):
    count = len(layout)
    pieces, (w_query, hidden_ref, queries_ref) = refs[:count], refs[count:]
    for piece, spots in zip(pieces, layout):
        taken = 0
        for start, size in spots:
            hidden_ref[start : start + size, :] = piece[taken : taken + size, :]
            taken += size
    queries = jnp.dot(hidden_ref[...], w_query[...], preferred_element_type=jnp.float32)
    queries_ref[...] = queries.astype(jnp.bfloat16)


def ask(pieces, layout, w_query):
    tokens, channels = sum(piece.shape[0] for piece in pieces), w_query.shape[0]
    whole = jax.ShapeDtypeStruct((tokens, channels), jnp.bfloat16)
    return pl.pallas_call(
        functools.partial(query_kernel, layout),
        out_shape=(whole, whole),
        in_specs=[IN_VMEM] * (len(pieces) + 1),
        out_specs=(IN_VMEM, IN_VMEM),
        compiler_params=pltpu.CompilerParams(vmem_limit_bytes=16 * 2**20),
        cost_estimate=QUICK,
        name="ask",
    )(*pieces, w_query)


def attend_kernel(piece_count, part_count, last, queries_ref, keyval_hbm, *refs):
    refs = list(refs)
    pieces = [refs.pop(0) for _ in range(piece_count)]
    parts = [[refs.pop(0) for _ in range(3)] for _ in range(part_count)]
    ending = [refs.pop(0) for _ in range(2)] if last else None
    new = [refs.pop(0) for _ in range(1 if last else 3)]
    w_keyval, w_out, keys, values, mixed, sems = refs
    tokens, channels = queries_ref.shape
    keyval_copy = pltpu.make_async_copy(keyval_hbm, w_keyval, sems.at[0])
    keyval_copy.start()
    if last:
        out_copy = pltpu.make_async_copy(ending[1], w_out, sems.at[1])
        out_copy.start()
    keyval_copy.wait()
    key_count = 0
    for piece in pieces:
        spot = slice(key_count, key_count + piece.shape[0])
        keyval = jnp.dot(piece[...], w_keyval[...], preferred_element_type=jnp.float32)
        keyval = keyval.astype(jnp.bfloat16)
        keys[spot, :] = keyval[:, :channels]
        values[spot, :] = keyval[:, channels:]
        key_count = spot.stop
    is_low = lax.broadcasted_iota(jnp.int32, (tokens, PAIR), 1) < HEAD_DIM
    ones = jnp.ones((key_count, PAIR), jnp.bfloat16)
    for start in range(0, channels, PAIR):
        lanes = slice(start, start + PAIR)
        both = queries_ref[:, lanes] * HEAD_DIM ** (-0.5)
        nothing = jnp.zeros_like(both)
        split = jnp.concatenate(
            [jnp.where(is_low, both, nothing), jnp.where(is_low, nothing, both)], axis=0
        )
        scores = lax.dot_general(
            split, keys[:, lanes], (((1,), (1,)), ((), ())), preferred_element_type=jnp.float32
        )
        best = jnp.max(scores, axis=1, keepdims=True)
        probability = jnp.exp(scores - best).astype(jnp.bfloat16)
        product = jnp.dot(
            probability,
            jnp.concatenate([values[:, lanes], ones], axis=1),
            preferred_element_type=jnp.float32,
        )
        best = jnp.where(is_low, best[:tokens], best[tokens:])
        weighted = jnp.where(is_low, product[:tokens, :PAIR], product[tokens:, :PAIR])
        total = jnp.where(is_low, product[:tokens, PAIR:], product[tokens:, PAIR:])
        if last:
            top = functools.reduce(jnp.maximum, [part[2][:, lanes] for part in parts], best)
            scale = jnp.exp(best - top)
            weighted, total = weighted * scale, total * scale
            for part in parts:
                scale = jnp.exp(part[2][:, lanes] - top)
                weighted = weighted + part[0][:, lanes] * scale
                total = total + part[1][:, lanes] * scale
            mixed[:, lanes] = (weighted / total).astype(jnp.bfloat16)
        else:
            new[0][:, lanes] = weighted
            new[1][:, lanes] = total
            new[2][:, lanes] = best
    if last:
        out_copy.wait()
        result = ending[0][...].astype(jnp.float32) + jnp.dot(
            mixed[...], w_out[...], preferred_element_type=jnp.float32
        )
        new[0][...] = result.astype(jnp.bfloat16)


def attend(queries, w_keyval, pieces, parts, ending, name):
    tokens, channels = queries.shape
    key_count = sum(piece.shape[0] for piece in pieces)
    last = ending is not None
    part = jax.ShapeDtypeStruct((tokens, channels), jnp.float32)
    whole = jax.ShapeDtypeStruct((tokens, channels), jnp.bfloat16)
    args = [queries, w_keyval, *pieces, *(array for each in parts for array in each), *(ending or ())]
    in_specs = [IN_VMEM] * len(args)
    in_specs[1] = IN_PLACE
    if last:
        in_specs[-1] = IN_PLACE
    return pl.pallas_call(
        functools.partial(attend_kernel, len(pieces), len(parts), last),
        out_shape=whole if last else (part,) * 3,
        in_specs=in_specs,
        out_specs=IN_VMEM if last else (IN_VMEM,) * 3,
        scratch_shapes=[
            pltpu.VMEM(w_keyval.shape, jnp.bfloat16),
            pltpu.VMEM((channels, channels), jnp.bfloat16),
            pltpu.VMEM((key_count, channels), jnp.bfloat16),
            pltpu.VMEM((key_count, channels), jnp.bfloat16),
            pltpu.VMEM((tokens, channels), jnp.bfloat16),
            pltpu.SemaphoreType.DMA((2,)),
        ],
        compiler_params=pltpu.CompilerParams(vmem_limit_bytes=VMEM_BYTES),
        cost_estimate=QUICK,
        name=name,
    )(*args)


def from_edges(block, axis):
    count = lax.axis_size(axis)
    forward = [(i, i + 1) for i in range(count - 1)]
    backward = [(target, source) for source, target in forward]
    low = lax.ppermute(block[:, -1], axis, forward)
    high = lax.ppermute(block[:, 0], axis, backward)
    return low, high


def permute(value, pairs):
    bands = lax.axis_size("band")
    flat = [(source[0] * bands + source[1], target[0] * bands + target[1]) for source, target in pairs]
    return lax.ppermute(value, ("frame", "band"), flat)


def ordered(value, *before):
    return lax.optimization_barrier((value, *before))[0]


def cast(own, before=()):
    frames, bands = lax.axis_size("frame"), lax.axis_size("band")
    columns = frames // 2
    reaches = [columns >> i for i in range(1, columns.bit_length())]
    direct = [
        permute(own, [((0, b), (2 * reach + b % 2, b)) for b in range(bands)]) for reach in reaches
    ]
    if direct:
        held = functools.reduce(jnp.add, lax.optimization_barrier((*direct, *before))[: len(direct)])
    else:
        held = jnp.zeros_like(own)
    for reach in reaches[1:]:
        relays = [
            ((2 * i + b % 2, b), (2 * (i + reach) + b % 2, b))
            for i in range(2 * reach, columns, 2 * reach)
            for b in range(bands)
        ]
        held = held + permute(held, relays)
    held = jnp.where(lax.axis_index("frame") == 0, own, held)
    holders = [(f, b) for f in range(2, frames) for b in range(bands) if f % 2 == b % 2]
    beside = permute(
        held,
        [((f, b), (f ^ 1, b)) for f, b in holders] + [((0, b), (1, b)) for b in range(bands)],
    )
    return held, beside


def swap(value, distance):
    frames, bands = lax.axis_size("frame"), lax.axis_size("band")
    return permute(value, [((f, b), (f, b ^ distance)) for f in range(frames) for b in range(bands)])


def sees_all(chunks, look):
    frames, bands = lax.axis_size("frame"), lax.axis_size("band")
    if frames % 2 or frames & (frames - 1) or bands != 4:
        pieces = [lax.all_gather(chunk, ("frame", "band"))[b] for chunk in chunks for b in range(bands)]
        return [], pieces
    held0, beside0 = cast(chunks[0], (chunks[1],))
    near0 = held0 + beside0
    near0_core, far0 = swap(near0, 1), swap(near0, 2)
    held1, beside1 = cast(chunks[1], (held0,))
    look0 = look([near0, ordered(near0_core, held1)])
    near1 = held1 + ordered(beside1, look0)
    near1_core, far1 = swap(near1, 1), swap(near1, 2)
    far0_core = swap(far0, 1)
    look1 = look([far0, ordered(far0_core, near1)])
    look2 = look([near1, ordered(near1_core, look1)])
    far1 = ordered(far1, look2)
    far1_core = swap(far1, 1)
    return [look0, look1, look2], [far1, far1_core]


def per_device(latents, conv_weight, conv_bias, w_query, w_keyval, w_out):
    frames, row_count, width, channels = latents.shape
    tokens = row_count * width
    half = row_count // 2
    taps_weight = conv_weight.reshape(3, 3 * channels, channels)
    inner = ((1, half),)
    outer = ((0, 1), (half + 1, row_count - half - 1))
    seam = (half + 1) * width
    layout = (((0, width), (seam, tokens - seam)), ((width, half * width),))
    low, high = from_edges(latents, "band")
    blocks = [latents[frame].reshape(tokens, channels) for frame in range(frames)]
    first, at_hand = convolve_inner(blocks[0], taps_weight, conv_bias, width, inner)
    parts = [
        convolve_outer(
            block, low[frame], high[frame], at_hand, conv_bias, first, width, inner, outer, frame > 0
        )
        for frame, block in enumerate(blocks)
    ]
    asked = [ask(part, layout, w_query) for part in parts]
    def look(pieces):
        return tuple(attend(queries, w_keyval, pieces, (), None, "attend") for _, queries in asked)

    looks, pieces = sees_all((first, parts[0][0]), look)
    results = [
        attend(queries, w_keyval, pieces, [each[i] for each in looks], (hidden, w_out), "join")
        for i, (hidden, queries) in enumerate(asked)
    ]
    return jnp.stack(results).reshape(latents.shape)


def solution(mesh):
    return jax.shard_map(
        per_device,
        mesh=mesh,
        in_specs=(P("frame", "band", None, None), P(), P(), P(), P(), P()),
        out_specs=P("frame", "band", None, None),
        check_vma=False,
    )
```

```python
import functools

import jax
import jax.numpy as jnp
from jax import lax
from jax.experimental import pallas as pl
from jax.experimental.pallas import tpu as pltpu
from jax.sharding import PartitionSpec as P

HEAD_DIM = 64
PAIR = 2 * HEAD_DIM
VMEM_BYTES = 40 * 2**20
CONV_VMEM_BYTES = 28 * 2**20
IN_VMEM = pl.BlockSpec(memory_space=pltpu.VMEM)
IN_PLACE = pl.BlockSpec(memory_space=pl.ANY)
IN_HBM = pl.BlockSpec(memory_space=pltpu.HBM)
SHIFTS = (1, 0, 2)
QUICK = pl.CostEstimate(flops=1, bytes_accessed=1, transcendentals=0)


def conv_span(width, spans, x_ref, low_ref, high_ref, weight, bias_ref, taps, waits=None):
    tokens, channels = x_ref.shape
    last_row = tokens // width
    blocks, starts, place = [], [], 0
    for first, count in spans:
        begin, end = max(first - 1, 0), min(first + count + 1, last_row)
        starts.append(place)
        if first == 0:
            blocks.append(low_ref[...])
        blocks.append(x_ref[begin * width : end * width, :])
        if first + count == last_row:
            blocks.append(high_ref[...])
        place += count + 2
    padded = place * width
    raw = (blocks[0] if len(blocks) == 1 else jnp.concatenate(blocks, axis=0)).astype(jnp.float32)
    active = raw * jax.nn.sigmoid(raw)
    column = lax.rem(lax.broadcasted_iota(jnp.int32, (padded, 1), 0), width)
    before = jnp.where(column == 0, 0.0, pltpu.roll(active, 1, 0))
    after = jnp.where(column == width - 1, 0.0, pltpu.roll(active, padded - 1, 0))
    taps[:padded, :channels] = before.astype(jnp.bfloat16)
    taps[:padded, channels : 2 * channels] = active.astype(jnp.bfloat16)
    taps[:padded, 2 * channels :] = after.astype(jnp.bfloat16)

    def joined(parts):
        return parts[0] if len(parts) == 1 else jnp.concatenate(parts, axis=0)

    own = joined([x_ref[first * width : (first + count) * width, :] for first, count in spans])
    total = own.astype(jnp.float32) + bias_ref[...].astype(jnp.float32)[None, :]
    for shift in SHIFTS:
        if waits:
            waits[shift].wait()
        rows = joined(
            [
                taps[(start + shift) * width : (start + shift + count) * width, :]
                for start, (_, count) in zip(starts, spans)
            ]
        )
        total = total + jnp.dot(rows, weight[shift], preferred_element_type=jnp.float32)
    return total.astype(jnp.bfloat16)


def inner_kernel(
    width, spans, x_hbm, weight_hbm, bias_hbm, out_ref, x_ref, top_ref, bottom_ref, weight, bias_ref, taps, sems
):
    x_copy = pltpu.make_async_copy(x_hbm, x_ref, sems.at[3])
    bias_copy = pltpu.make_async_copy(bias_hbm, bias_ref, sems.at[4])
    copies = [
        pltpu.make_async_copy(weight_hbm.at[shift], weight.at[shift], sems.at[shift])
        for shift in range(3)
    ]
    is_source = lax.axis_index("frame") == 0
    x_copy.start()

    @pl.when(is_source)
    def _():
        bias_copy.start()
        for shift in SHIFTS:
            copies[shift].start()

    x_copy.wait()
    top_ref[...] = x_ref[:width, :]
    bottom_ref[...] = x_ref[x_ref.shape[0] - width :, :]

    @pl.when(is_source)
    def _():
        bias_copy.wait()
        out_ref[...] = conv_span(width, spans, x_ref, None, None, weight, bias_ref, taps, copies)


def outer_kernel(
    width, outer, x_ref, low_ref, high_ref, weight, bias_ref, out_ref, taps
):
    def compute(spans):
        return conv_span(width, spans, x_ref, low_ref, high_ref, weight, bias_ref, taps)

    @pl.when(lax.axis_index("frame") == 0)
    def _():
        out_ref[...] = compute(outer)


def convolve_inner(x, taps_weight, bias, width, inner):
    channels = x.shape[1]
    made = sum(count for _, count in inner)
    part = jax.ShapeDtypeStruct((width, channels), jnp.bfloat16)
    return pl.pallas_call(
        functools.partial(inner_kernel, width, inner),
        out_shape=(
            jax.ShapeDtypeStruct((made * width, channels), jnp.bfloat16),
            pltpu.VMEM(x.shape, jnp.bfloat16),
            part,
            part,
            pltpu.VMEM(taps_weight.shape, jnp.bfloat16),
            pltpu.VMEM(bias.shape, jnp.bfloat16),
        ),
        in_specs=[IN_HBM] * 3,
        out_specs=(IN_VMEM,) * 6,
        scratch_shapes=[
            pltpu.VMEM(((made + 2 * len(inner)) * width, 3 * channels), jnp.bfloat16),
            pltpu.SemaphoreType.DMA((5,)),
        ],
        compiler_params=pltpu.CompilerParams(vmem_limit_bytes=CONV_VMEM_BYTES),
        cost_estimate=QUICK,
        name="inner",
    )(*(pltpu.with_memory_space_constraint(each, pltpu.HBM) for each in (x, taps_weight, bias)))


def padded_rows(*many):
    return max(sum(count + 2 for _, count in spans) for spans in many)


def convolve_outer(x, low, high, weight, bias, width, outer):
    channels = x.shape[1]
    made = sum(count for _, count in outer)
    return pl.pallas_call(
        functools.partial(outer_kernel, width, outer),
        out_shape=jax.ShapeDtypeStruct((made * width, channels), jnp.bfloat16),
        in_specs=[IN_VMEM] * 5,
        out_specs=IN_VMEM,
        scratch_shapes=[pltpu.VMEM((padded_rows(outer) * width, 3 * channels), jnp.bfloat16)],
        compiler_params=pltpu.CompilerParams(vmem_limit_bytes=CONV_VMEM_BYTES),
        cost_estimate=QUICK,
        name="outer",
    )(x, low, high, *(pltpu.with_memory_space_constraint(each, pltpu.VMEM) for each in (weight, bias)))


def ask_kernel(
    width, spans, layout, w_query, x_ref, low_ref, high_ref, weight, bias_ref, *refs
):
    pieces, (hidden_ref, queries_ref, taps) = refs[:-3], refs[-3:]

    def lay(values):
        for value, spots in zip(values, layout):
            taken = 0
            for start, size in spots:
                hidden_ref[start : start + size, :] = value[taken : taken + size, :]
                taken += size

    def compute():
        for each, spots in zip(spans, layout):
            lay_one = conv_span(width, each, x_ref, low_ref, high_ref, weight, bias_ref, taps)
            taken = 0
            for start, size in spots:
                hidden_ref[start : start + size, :] = lay_one[taken : taken + size]
                taken += size

    if pieces:
        pl.when(lax.axis_index("frame") == 0)(lambda: lay(pieces))
        pl.when(lax.axis_index("frame") != 0)(compute)
    else:
        compute()
    queries = jnp.dot(hidden_ref[...], w_query[...], preferred_element_type=jnp.float32)
    queries_ref[...] = queries.astype(jnp.bfloat16)


def ask(pieces, x, low, high, weight, bias, w_query, width, spans, layout):
    channels = x.shape[1]
    whole = jax.ShapeDtypeStruct(x.shape, jnp.bfloat16)
    return pl.pallas_call(
        functools.partial(ask_kernel, width, spans, layout),
        out_shape=(whole, whole),
        in_specs=[IN_VMEM] * (len(pieces) + 6),
        out_specs=(IN_VMEM, IN_VMEM),
        scratch_shapes=[pltpu.VMEM((padded_rows(*spans) * width, 3 * channels), jnp.bfloat16)],
        compiler_params=pltpu.CompilerParams(vmem_limit_bytes=CONV_VMEM_BYTES),
        cost_estimate=QUICK,
        name="ask",
    )(w_query, x, low, high, weight, bias, *pieces)


def attend_kernel(piece_count, part_count, last, queries_ref, keyval_hbm, *refs):
    refs = list(refs)
    pieces = [refs.pop(0) for _ in range(piece_count)]
    parts = [[refs.pop(0) for _ in range(3)] for _ in range(part_count)]
    ending = [refs.pop(0) for _ in range(2)] if last else None
    new = [refs.pop(0) for _ in range(1 if last else 3)]
    w_keyval, w_out, keys, values, mixed, sems = refs
    tokens, channels = queries_ref.shape
    keyval_copy = pltpu.make_async_copy(keyval_hbm, w_keyval, sems.at[0])
    keyval_copy.start()
    if last:
        out_copy = pltpu.make_async_copy(ending[1], w_out, sems.at[1])
        out_copy.start()
    keyval_copy.wait()
    key_count = 0
    for piece in pieces:
        spot = slice(key_count, key_count + piece.shape[0])
        keyval = jnp.dot(piece[...], w_keyval[...], preferred_element_type=jnp.float32)
        keyval = keyval.astype(jnp.bfloat16)
        keys[spot, :] = keyval[:, :channels]
        values[spot, :] = keyval[:, channels:]
        key_count = spot.stop
    is_low = lax.broadcasted_iota(jnp.int32, (tokens, PAIR), 1) < HEAD_DIM
    ones = jnp.ones((key_count, PAIR), jnp.bfloat16)
    for start in range(0, channels, PAIR):
        lanes = slice(start, start + PAIR)
        both = queries_ref[:, lanes] * HEAD_DIM ** (-0.5)
        nothing = jnp.zeros_like(both)
        split = jnp.concatenate(
            [jnp.where(is_low, both, nothing), jnp.where(is_low, nothing, both)], axis=0
        )
        scores = lax.dot_general(
            split, keys[:, lanes], (((1,), (1,)), ((), ())), preferred_element_type=jnp.float32
        )
        best = jnp.max(scores, axis=1, keepdims=True)
        probability = jnp.exp(scores - best).astype(jnp.bfloat16)
        product = jnp.dot(
            probability,
            jnp.concatenate([values[:, lanes], ones], axis=1),
            preferred_element_type=jnp.float32,
        )
        best = jnp.where(is_low, best[:tokens], best[tokens:])
        weighted = jnp.where(is_low, product[:tokens, :PAIR], product[tokens:, :PAIR])
        total = jnp.where(is_low, product[:tokens, PAIR:], product[tokens:, PAIR:])
        if last:
            top = functools.reduce(jnp.maximum, [part[2][:, lanes] for part in parts], best)
            scale = jnp.exp(best - top)
            weighted, total = weighted * scale, total * scale
            for part in parts:
                scale = jnp.exp(part[2][:, lanes] - top)
                weighted = weighted + part[0][:, lanes] * scale
                total = total + part[1][:, lanes] * scale
            mixed[:, lanes] = (weighted / total).astype(jnp.bfloat16)
        else:
            new[0][:, lanes] = weighted
            new[1][:, lanes] = total
            new[2][:, lanes] = best
    if last:
        out_copy.wait()
        result = ending[0][...].astype(jnp.float32) + jnp.dot(
            mixed[...], w_out[...], preferred_element_type=jnp.float32
        )
        new[0][...] = result.astype(jnp.bfloat16)


def attend(queries, w_keyval, pieces, parts, ending, name):
    tokens, channels = queries.shape
    key_count = sum(piece.shape[0] for piece in pieces)
    last = ending is not None
    part = jax.ShapeDtypeStruct((tokens, channels), jnp.float32)
    whole = jax.ShapeDtypeStruct((tokens, channels), jnp.bfloat16)
    args = [queries, w_keyval, *pieces, *(array for each in parts for array in each), *(ending or ())]
    in_specs = [IN_VMEM] * len(args)
    in_specs[1] = IN_PLACE
    if last:
        in_specs[-1] = IN_PLACE
    return pl.pallas_call(
        functools.partial(attend_kernel, len(pieces), len(parts), last),
        out_shape=whole if last else (part,) * 3,
        in_specs=in_specs,
        out_specs=IN_VMEM if last else (IN_VMEM,) * 3,
        scratch_shapes=[
            pltpu.VMEM(w_keyval.shape, jnp.bfloat16),
            pltpu.VMEM((channels, channels), jnp.bfloat16),
            pltpu.VMEM((key_count, channels), jnp.bfloat16),
            pltpu.VMEM((key_count, channels), jnp.bfloat16),
            pltpu.VMEM((tokens, channels), jnp.bfloat16),
            pltpu.SemaphoreType.DMA((2,)),
        ],
        compiler_params=pltpu.CompilerParams(vmem_limit_bytes=VMEM_BYTES),
        cost_estimate=QUICK,
        name=name,
    )(*args)


def from_edges(top, bottom):
    count = lax.axis_size("band")
    forward = [(i, i + 1) for i in range(count - 1)]
    backward = [(target, source) for source, target in forward]
    return lax.ppermute(bottom, "band", forward), lax.ppermute(top, "band", backward)


def permute(value, pairs):
    bands = lax.axis_size("band")
    flat = [(source[0] * bands + source[1], target[0] * bands + target[1]) for source, target in pairs]
    return lax.ppermute(value, ("frame", "band"), flat)


def ordered(value, *before):
    return lax.optimization_barrier((value, *before))[0]


def step_across(own, is_source, before=()):
    pairs = [((0, b), (1, b)) for b in range(lax.axis_size("band")) if b % 2]
    if lax.axis_size("frame") == 1:
        return own
    return jnp.where(is_source, own, ordered(permute(own, pairs), *before))


def cast(roots, before=()):
    frames, bands = lax.axis_size("frame"), lax.axis_size("band")
    places = frames // 2
    held, reach = list(roots), places
    while reach > 1:
        reach //= 2
        pairs = [
            ((2 * i + b % 2, b), (2 * (i + reach) + b % 2, b))
            for i in range(0, places, 2 * reach)
            for b in range(bands)
        ]
        arrived = [permute(each, pairs) for each in held]
        if before:
            arrived[0] = ordered(arrived[0], *before)
        held = [have + new for have, new in zip(held, arrived)]
        before = ()
    return held


def exchange(held):
    frames, bands = lax.axis_size("frame"), lax.axis_size("band")
    holders = [(f, b) for f in range(frames) for b in range(bands) if f % 2 == b % 2]
    beside = permute(held, [((f, b), (f ^ 1, b)) for f, b in holders if f != 1])
    far = permute(
        held,
        [((f, b), (f, b ^ 2)) for f, b in holders] + [((0, b), (0, b ^ 2)) for b in range(bands) if b % 2],
    )
    diagonal = permute(held, [((f, b), (f ^ 1, b ^ 2)) for f, b in holders if f != 1])
    return beside, far, diagonal


def swap_cores(value):
    frames, bands = lax.axis_size("frame"), lax.axis_size("band")
    return permute(value, [((f, b), (f, b ^ 1)) for f in range(frames) for b in range(bands)])


def own_side(held, parts):
    beside, far, diagonal = parts
    return [held + beside, far + diagonal]


def sees_all(chunks, starts, look, early):
    frames, bands = lax.axis_size("frame"), lax.axis_size("band")
    if frames < 2 or frames & (frames - 1) or bands != 4:
        pieces = [lax.all_gather(chunk, ("frame", "band"))[b] for chunk in chunks for b in range(bands)]
        return [], pieces
    held0, held1 = cast(starts, (*early, starts[1]))
    parts0 = exchange(held0)
    held1 = ordered(held1, held0)
    parts1 = exchange(held1)
    here0 = own_side(held0, ordered(parts0, held1))
    there0 = [swap_cores(piece) for piece in here0]
    look0 = look(here0)
    here1 = own_side(held1, ordered(parts1, look0))
    look1 = look(ordered(there0, look0, here1))
    there1 = [swap_cores(piece) for piece in here1]
    look2 = look(ordered(here1, look1))
    return [look0, look1, look2], ordered(there1, look2)


def per_device(latents, conv_weight, conv_bias, w_query, w_keyval, w_out):
    frames, row_count, width, channels = latents.shape
    tokens = row_count * width
    half = row_count // 2
    taps_weight = conv_weight.reshape(3, 3 * channels, channels)
    inner = ((1, half),)
    outer = ((0, 1), (half + 1, row_count - half - 1))
    seam = (half + 1) * width
    layout = (((0, width), (seam, tokens - seam)), ((width, half * width),))
    latents, is_source = lax.optimization_barrier((latents, lax.axis_index("frame") == 0))
    blocks = [latents[frame].reshape(tokens, channels) for frame in range(frames)]
    first, at_hand, top, bottom, *weight_bias = convolve_inner(
        blocks[0], taps_weight, conv_bias, width, inner
    )
    low, high = from_edges(top, bottom)
    begun = step_across(first, is_source, (low, high))
    second = convolve_outer(at_hand, low, high, *weight_bias, width, outer)
    asked = [
        ask((second, first), at_hand, low, high, taps_weight, conv_bias, w_query, width, (outer, inner), layout)
    ]
    for block in blocks[1:]:
        edges = from_edges(block[:width], block[-width:])
        asked.append(ask((), block, *edges, taps_weight, conv_bias, w_query, width, (outer, inner), layout))
    chunks = (first, second)
    starts = (begun, step_across(second, is_source))

    def look(pieces):
        return tuple(attend(queries, w_keyval, pieces, (), None, "attend") for _, queries in asked)

    looks, pieces = sees_all(chunks, starts, look, [queries for _, queries in asked])
    results = [
        attend(queries, w_keyval, pieces, [each[i] for each in looks], (hidden, w_out), "join")
        for i, (hidden, queries) in enumerate(asked)
    ]
    return jnp.stack(results).reshape(latents.shape)


def solution(mesh):
    return jax.shard_map(
        per_device,
        mesh=mesh,
        in_specs=(P("frame", "band", None, None), P(), P(), P(), P(), P()),
        out_specs=P("frame", "band", None, None),
        check_vma=False,
    )
```

```python
import functools

import jax
import jax.numpy as jnp
from jax import lax
from jax.experimental import pallas as pl
from jax.experimental.pallas import tpu as pltpu
from jax.sharding import PartitionSpec as P

HEAD_DIM = 64
PAIR = 2 * HEAD_DIM
VMEM_BYTES = 36 * 2**20
CONV_VMEM_BYTES = 28 * 2**20
IN_VMEM = pl.BlockSpec(memory_space=pltpu.VMEM)
IN_PLACE = pl.BlockSpec(memory_space=pl.ANY)
IN_HBM = pl.BlockSpec(memory_space=pltpu.HBM)
SHIFTS = (1, 0, 2)
QUICK = pl.CostEstimate(flops=1, bytes_accessed=1, transcendentals=0)


def conv_span(width, spans, x_ref, low_ref, high_ref, weight, bias_ref, taps, waits=None):
    tokens, channels = x_ref.shape
    last_row = tokens // width
    blocks, starts, place = [], [], 0
    for first, count in spans:
        begin, end = max(first - 1, 0), min(first + count + 1, last_row)
        starts.append(place)
        if first == 0:
            blocks.append(low_ref[...])
        blocks.append(x_ref[begin * width : end * width, :])
        if first + count == last_row:
            blocks.append(high_ref[...])
        place += count + 2
    padded = place * width
    raw = (blocks[0] if len(blocks) == 1 else jnp.concatenate(blocks, axis=0)).astype(jnp.float32)
    active = raw * jax.nn.sigmoid(raw)
    column = lax.rem(lax.broadcasted_iota(jnp.int32, (padded, 1), 0), width)
    before = jnp.where(column == 0, 0.0, pltpu.roll(active, 1, 0))
    after = jnp.where(column == width - 1, 0.0, pltpu.roll(active, padded - 1, 0))
    taps[:padded, :channels] = before.astype(jnp.bfloat16)
    taps[:padded, channels : 2 * channels] = active.astype(jnp.bfloat16)
    taps[:padded, 2 * channels :] = after.astype(jnp.bfloat16)

    def joined(parts):
        return parts[0] if len(parts) == 1 else jnp.concatenate(parts, axis=0)

    own = joined([x_ref[first * width : (first + count) * width, :] for first, count in spans])
    total = own.astype(jnp.float32) + bias_ref[...].astype(jnp.float32)[None, :]
    for shift in SHIFTS:
        if waits:
            waits[shift].wait()
        rows = joined(
            [
                taps[(start + shift) * width : (start + shift + count) * width, :]
                for start, (_, count) in zip(starts, spans)
            ]
        )
        total = total + jnp.dot(rows, weight[shift], preferred_element_type=jnp.float32)
    return total.astype(jnp.bfloat16)


def inner_kernel(
    width, spans, x_hbm, weight_hbm, bias_hbm, out_ref, x_ref, top_ref, bottom_ref, weight, bias_ref, taps, sems
):
    x_copy = pltpu.make_async_copy(x_hbm, x_ref, sems.at[3])
    bias_copy = pltpu.make_async_copy(bias_hbm, bias_ref, sems.at[4])
    copies = [
        pltpu.make_async_copy(weight_hbm.at[shift], weight.at[shift], sems.at[shift])
        for shift in range(3)
    ]
    is_source = lax.axis_index("frame") == 0
    x_copy.start()

    @pl.when(is_source)
    def _():
        bias_copy.start()
        for shift in SHIFTS:
            copies[shift].start()

    x_copy.wait()
    top_ref[...] = x_ref[:width, :]
    bottom_ref[...] = x_ref[x_ref.shape[0] - width :, :]

    @pl.when(is_source)
    def _():
        bias_copy.wait()
        out_ref[...] = conv_span(width, spans, x_ref, None, None, weight, bias_ref, taps, copies)


def outer_kernel(
    width, outer, x_ref, low_ref, high_ref, weight, bias_ref, out_ref, taps
):
    def compute(spans):
        return conv_span(width, spans, x_ref, low_ref, high_ref, weight, bias_ref, taps)

    @pl.when(lax.axis_index("frame") == 0)
    def _():
        out_ref[...] = compute(outer)


def convolve_inner(x, taps_weight, bias, width, inner):
    channels = x.shape[1]
    made = sum(count for _, count in inner)
    part = jax.ShapeDtypeStruct((width, channels), jnp.bfloat16)
    return pl.pallas_call(
        functools.partial(inner_kernel, width, inner),
        out_shape=(
            jax.ShapeDtypeStruct((made * width, channels), jnp.bfloat16),
            pltpu.VMEM(x.shape, jnp.bfloat16),
            part,
            part,
            pltpu.VMEM(taps_weight.shape, jnp.bfloat16),
            pltpu.VMEM(bias.shape, jnp.bfloat16),
        ),
        in_specs=[IN_HBM] * 3,
        out_specs=(IN_VMEM,) * 6,
        scratch_shapes=[
            pltpu.VMEM(((made + 2 * len(inner)) * width, 3 * channels), jnp.bfloat16),
            pltpu.SemaphoreType.DMA((5,)),
        ],
        compiler_params=pltpu.CompilerParams(vmem_limit_bytes=CONV_VMEM_BYTES),
        cost_estimate=QUICK,
        name="inner",
    )(*(pltpu.with_memory_space_constraint(each, pltpu.HBM) for each in (x, taps_weight, bias)))


def padded_rows(*many):
    return max(sum(count + 2 for _, count in spans) for spans in many)


def convolve_outer(x, low, high, weight, bias, width, outer):
    channels = x.shape[1]
    made = sum(count for _, count in outer)
    return pl.pallas_call(
        functools.partial(outer_kernel, width, outer),
        out_shape=jax.ShapeDtypeStruct((made * width, channels), jnp.bfloat16),
        in_specs=[IN_VMEM] * 5,
        out_specs=IN_VMEM,
        scratch_shapes=[pltpu.VMEM((padded_rows(outer) * width, 3 * channels), jnp.bfloat16)],
        compiler_params=pltpu.CompilerParams(vmem_limit_bytes=CONV_VMEM_BYTES),
        cost_estimate=QUICK,
        name="outer",
    )(x, low, high, *(pltpu.with_memory_space_constraint(each, pltpu.VMEM) for each in (weight, bias)))


def ask_kernel(
    width, spans, layout, w_query, x_ref, low_ref, high_ref, weight, bias_ref, *refs
):
    pieces, (hidden_ref, queries_ref, taps) = refs[:-3], refs[-3:]

    def lay(values):
        for value, spots in zip(values, layout):
            taken = 0
            for start, size in spots:
                hidden_ref[start : start + size, :] = value[taken : taken + size, :]
                taken += size

    def compute():
        for each, spots in zip(spans, layout):
            lay_one = conv_span(width, each, x_ref, low_ref, high_ref, weight, bias_ref, taps)
            taken = 0
            for start, size in spots:
                hidden_ref[start : start + size, :] = lay_one[taken : taken + size]
                taken += size

    if pieces:
        pl.when(lax.axis_index("frame") == 0)(lambda: lay(pieces))
        pl.when(lax.axis_index("frame") != 0)(compute)
    else:
        compute()
    queries = jnp.dot(hidden_ref[...], w_query[...], preferred_element_type=jnp.float32)
    queries_ref[...] = queries.astype(jnp.bfloat16)


def ask(pieces, x, low, high, weight, bias, w_query, width, spans, layout):
    channels = x.shape[1]
    whole = jax.ShapeDtypeStruct(x.shape, jnp.bfloat16)
    return pl.pallas_call(
        functools.partial(ask_kernel, width, spans, layout),
        out_shape=(whole, whole),
        in_specs=[IN_VMEM] * (len(pieces) + 6),
        out_specs=(IN_VMEM, IN_VMEM),
        scratch_shapes=[pltpu.VMEM((padded_rows(*spans) * width, 3 * channels), jnp.bfloat16)],
        compiler_params=pltpu.CompilerParams(vmem_limit_bytes=CONV_VMEM_BYTES),
        cost_estimate=QUICK,
        name="ask",
    )(w_query, x, low, high, weight, bias, *pieces)


def attend_kernel(piece_count, part_count, last, queries_ref, w_keyval, *refs):
    refs = list(refs)
    pieces = [refs.pop(0) for _ in range(piece_count)]
    parts = [[refs.pop(0) for _ in range(3)] for _ in range(part_count)]
    ending = [refs.pop(0) for _ in range(2)] if last else None
    new = [refs.pop(0) for _ in range(1 if last else 3)]
    keys, values, mixed, joined = refs
    tokens, channels = queries_ref.shape
    all_lanes = [slice(start, start + PAIR) for start in range(0, channels, PAIR)]
    if parts:
        for lanes in all_lanes:
            top = functools.reduce(jnp.maximum, [part[2][:, lanes] for part in parts])
            scales = [jnp.exp(part[2][:, lanes] - top) for part in parts]
            for i in range(2):
                scaled = [part[i][:, lanes] * scale for part, scale in zip(parts, scales)]
                joined[i, :, lanes] = functools.reduce(jnp.add, scaled)
            joined[2, :, lanes] = top
    key_count = 0
    for piece in pieces:
        spot = slice(key_count, key_count + piece.shape[0])
        keyval = jnp.dot(piece[...], w_keyval[...], preferred_element_type=jnp.float32)
        keyval = keyval.astype(jnp.bfloat16)
        keys[spot, :] = keyval[:, :channels]
        values[spot, :] = keyval[:, channels:]
        key_count = spot.stop
    is_low = lax.broadcasted_iota(jnp.int32, (tokens, PAIR), 1) < HEAD_DIM
    ones = jnp.ones((key_count, PAIR), jnp.bfloat16)

    def scores_of(lanes):
        both = queries_ref[:, lanes] * HEAD_DIM ** (-0.5)
        nothing = jnp.zeros_like(both)
        split = jnp.concatenate(
            [jnp.where(is_low, both, nothing), jnp.where(is_low, nothing, both)], axis=0
        )
        return lax.dot_general(
            split, keys[:, lanes], (((1,), (1,)), ((), ())), preferred_element_type=jnp.float32
        )

    next_scores = scores_of(all_lanes[0])
    for lanes, next_lanes in zip(all_lanes, all_lanes[1:] + [None]):
        scores = next_scores
        if next_lanes is not None:
            next_scores = scores_of(next_lanes)
        best = jnp.max(scores, axis=1, keepdims=True)
        probability = jnp.exp(scores - best).astype(jnp.bfloat16)
        product = jnp.dot(
            probability,
            jnp.concatenate([values[:, lanes], ones], axis=1),
            preferred_element_type=jnp.float32,
        )
        best = jnp.where(is_low, best[:tokens], best[tokens:])
        weighted = jnp.where(is_low, product[:tokens, :PAIR], product[tokens:, :PAIR])
        total = jnp.where(is_low, product[:tokens, PAIR:], product[tokens:, PAIR:])
        if parts:
            top = jnp.maximum(best, joined[2, :, lanes])
            scale, old_scale = jnp.exp(best - top), jnp.exp(joined[2, :, lanes] - top)
            weighted = weighted * scale + joined[0, :, lanes] * old_scale
            total = total * scale + joined[1, :, lanes] * old_scale
        if last:
            mixed[:, lanes] = (weighted / total).astype(jnp.bfloat16)
        else:
            new[0][:, lanes] = weighted
            new[1][:, lanes] = total
            new[2][:, lanes] = best
    if last:
        result = ending[0][...].astype(jnp.float32) + jnp.dot(
            mixed[...], ending[1][...], preferred_element_type=jnp.float32
        )
        new[0][...] = result.astype(jnp.bfloat16)


def attend(queries, w_keyval, pieces, parts, ending, name):
    tokens, channels = queries.shape
    key_count = sum(piece.shape[0] for piece in pieces)
    last = ending is not None
    part = jax.ShapeDtypeStruct((tokens, channels), jnp.float32)
    whole = jax.ShapeDtypeStruct((tokens, channels), jnp.bfloat16)
    args = [queries, w_keyval, *pieces, *(array for each in parts for array in each), *(ending or ())]
    return pl.pallas_call(
        functools.partial(attend_kernel, len(pieces), len(parts), last),
        out_shape=whole if last else (part,) * 3,
        in_specs=[IN_VMEM] * len(args),
        out_specs=IN_VMEM if last else (IN_VMEM,) * 3,
        scratch_shapes=[
            pltpu.VMEM((key_count, channels), jnp.bfloat16),
            pltpu.VMEM((key_count, channels), jnp.bfloat16),
            pltpu.VMEM((tokens, channels), jnp.bfloat16),
            pltpu.VMEM((3, tokens, channels) if parts else (3, 8, PAIR), jnp.float32),
        ],
        compiler_params=pltpu.CompilerParams(vmem_limit_bytes=VMEM_BYTES),
        cost_estimate=QUICK,
        name=name,
    )(*args)


def from_edges(top, bottom):
    count = lax.axis_size("band")
    forward = [(i, i + 1) for i in range(count - 1)]
    backward = [(target, source) for source, target in forward]
    return lax.ppermute(bottom, "band", forward), lax.ppermute(top, "band", backward)


def permute(value, pairs):
    bands = lax.axis_size("band")
    flat = [(source[0] * bands + source[1], target[0] * bands + target[1]) for source, target in pairs]
    return lax.ppermute(value, ("frame", "band"), flat)


def ordered(value, *before):
    return lax.optimization_barrier((value, *before))[0]


def step_across(own, is_source, before=()):
    pairs = [((0, b), (1, b)) for b in range(lax.axis_size("band")) if b % 2]
    if lax.axis_size("frame") == 1:
        return own
    return jnp.where(is_source, own, ordered(permute(own, pairs), *before))


def cast(roots, before=()):
    frames, bands = lax.axis_size("frame"), lax.axis_size("band")
    places = frames // 2
    held, reach = list(roots), places
    while reach > 1:
        reach //= 2
        pairs = [
            ((2 * i + b % 2, b), (2 * (i + reach) + b % 2, b))
            for i in range(0, places, 2 * reach)
            for b in range(bands)
        ]
        arrived = [permute(each, pairs) for each in held]
        if before:
            arrived[0] = ordered(arrived[0], *before)
        held = [have + new for have, new in zip(held, arrived)]
        before = ()
    return held


def exchange(held):
    frames, bands = lax.axis_size("frame"), lax.axis_size("band")
    holders = [(f, b) for f in range(frames) for b in range(bands) if f % 2 == b % 2]
    diagonal = permute(held, [((f, b), (f ^ 1, b ^ 2)) for f, b in holders if f != 1])
    beside = permute(held, [((f, b), (f ^ 1, b)) for f, b in holders if f != 1])
    far = permute(
        held,
        [((f, b), (f, b ^ 2)) for f, b in holders] + [((0, b), (0, b ^ 2)) for b in range(bands) if b % 2],
    )
    return beside, diagonal, far


def swap_cores(value):
    frames, bands = lax.axis_size("frame"), lax.axis_size("band")
    return permute(value, [((f, b), (f, b ^ 1)) for f in range(frames) for b in range(bands)])


def own_side(held, parts):
    beside, diagonal, far = parts
    return [held + beside, far + diagonal]


def sees_all(chunks, starts, look, early):
    frames, bands = lax.axis_size("frame"), lax.axis_size("band")
    if frames < 2 or frames & (frames - 1) or bands != 4:
        pieces = [lax.all_gather(chunk, ("frame", "band"))[b] for chunk in chunks for b in range(bands)]
        return [], pieces
    held0, held1 = cast(starts, (*early, starts[1]))
    parts0 = exchange(held0)
    held1 = ordered(held1, held0)
    parts1 = exchange(held1)
    here0 = own_side(held0, ordered(parts0, held1))
    there0 = [swap_cores(piece) for piece in here0]
    look0 = look(here0)
    here1 = own_side(held1, ordered(parts1, look0))
    look1 = look(ordered(there0, look0, here1))
    there1 = [swap_cores(piece) for piece in here1]
    look2 = look(ordered(here1, look1))
    return [look0, look1, look2], ordered(there1, look2)


def per_device(latents, conv_weight, conv_bias, w_query, w_keyval, w_out):
    frames, row_count, width, channels = latents.shape
    tokens = row_count * width
    half = row_count // 2
    taps_weight = conv_weight.reshape(3, 3 * channels, channels)
    inner = ((1, half),)
    outer = ((0, 1), (half + 1, row_count - half - 1))
    seam = (half + 1) * width
    layout = (((0, width), (seam, tokens - seam)), ((width, half * width),))
    latents, is_source = lax.optimization_barrier((latents, lax.axis_index("frame") == 0))
    blocks = [latents[frame].reshape(tokens, channels) for frame in range(frames)]
    first, at_hand, top, bottom, *weight_bias = convolve_inner(
        blocks[0], taps_weight, conv_bias, width, inner
    )
    low, high = from_edges(top, bottom)
    begun = step_across(first, is_source, (low, high))
    second = convolve_outer(at_hand, low, high, *weight_bias, width, outer)
    asked = [
        ask((second, first), at_hand, low, high, taps_weight, conv_bias, w_query, width, (outer, inner), layout)
    ]
    for block in blocks[1:]:
        edges = from_edges(block[:width], block[-width:])
        asked.append(ask((), block, *edges, taps_weight, conv_bias, w_query, width, (outer, inner), layout))
    chunks = (first, second)
    starts = (begun, step_across(second, is_source))

    def look(pieces):
        return tuple(attend(queries, w_keyval, pieces, (), None, "attend") for _, queries in asked)

    looks, pieces = sees_all(chunks, starts, look, [queries for _, queries in asked])
    results = [
        attend(queries, w_keyval, pieces, [each[i] for each in looks], (hidden, w_out), "join")
        for i, (hidden, queries) in enumerate(asked)
    ]
    return jnp.stack(results).reshape(latents.shape)


def solution(mesh):
    return jax.shard_map(
        per_device,
        mesh=mesh,
        in_specs=(P("frame", "band", None, None), P(), P(), P(), P(), P()),
        out_specs=P("frame", "band", None, None),
        check_vma=False,
    )
```

```python
import functools

import jax
import jax.numpy as jnp
from jax import lax
from jax.experimental import pallas as pl
from jax.experimental.pallas import tpu as pltpu
from jax.sharding import PartitionSpec as P

HEAD_DIM = 64
PAIR = 2 * HEAD_DIM
VMEM_BYTES = 36 * 2**20
CONV_VMEM_BYTES = 28 * 2**20
IN_VMEM = pl.BlockSpec(memory_space=pltpu.VMEM)
IN_PLACE = pl.BlockSpec(memory_space=pl.ANY)
IN_HBM = pl.BlockSpec(memory_space=pltpu.HBM)
SHIFTS = (1, 0, 2)
QUICK = pl.CostEstimate(flops=1, bytes_accessed=1, transcendentals=0)


def conv_span(width, spans, x_ref, low_ref, high_ref, weight, bias_ref, taps, waits=None):
    tokens, channels = x_ref.shape
    last_row = tokens // width
    blocks, starts, place = [], [], 0
    for first, count in spans:
        begin, end = max(first - 1, 0), min(first + count + 1, last_row)
        starts.append(place)
        if first == 0:
            blocks.append(low_ref[...])
        blocks.append(x_ref[begin * width : end * width, :])
        if first + count == last_row:
            blocks.append(high_ref[...])
        place += count + 2
    padded = place * width
    raw = (blocks[0] if len(blocks) == 1 else jnp.concatenate(blocks, axis=0)).astype(jnp.float32)
    active = raw * jax.nn.sigmoid(raw)
    column = lax.rem(lax.broadcasted_iota(jnp.int32, (padded, 1), 0), width)
    before = jnp.where(column == 0, 0.0, pltpu.roll(active, 1, 0))
    after = jnp.where(column == width - 1, 0.0, pltpu.roll(active, padded - 1, 0))
    taps[:padded, :channels] = before.astype(jnp.bfloat16)
    taps[:padded, channels : 2 * channels] = active.astype(jnp.bfloat16)
    taps[:padded, 2 * channels :] = after.astype(jnp.bfloat16)

    def joined(parts):
        return parts[0] if len(parts) == 1 else jnp.concatenate(parts, axis=0)

    own = joined([x_ref[first * width : (first + count) * width, :] for first, count in spans])
    total = own.astype(jnp.float32) + bias_ref[...].astype(jnp.float32)[None, :]
    for shift in SHIFTS:
        if waits:
            waits[shift].wait()
        rows = joined(
            [
                taps[(start + shift) * width : (start + shift + count) * width, :]
                for start, (_, count) in zip(starts, spans)
            ]
        )
        total = total + jnp.dot(rows, weight[shift], preferred_element_type=jnp.float32)
    return total.astype(jnp.bfloat16)


def inner_kernel(
    width, spans, x_hbm, weight_hbm, bias_hbm, out_ref, x_ref, top_ref, bottom_ref, weight, bias_ref, taps, sems
):
    x_copy = pltpu.make_async_copy(x_hbm, x_ref, sems.at[3])
    bias_copy = pltpu.make_async_copy(bias_hbm, bias_ref, sems.at[4])
    copies = [
        pltpu.make_async_copy(weight_hbm.at[shift], weight.at[shift], sems.at[shift])
        for shift in range(3)
    ]
    is_source = lax.axis_index("frame") == 0
    x_copy.start()

    @pl.when(is_source)
    def _():
        bias_copy.start()
        for shift in SHIFTS:
            copies[shift].start()

    x_copy.wait()
    top_ref[...] = x_ref[:width, :]
    bottom_ref[...] = x_ref[x_ref.shape[0] - width :, :]

    @pl.when(is_source)
    def _():
        bias_copy.wait()
        out_ref[...] = conv_span(width, spans, x_ref, None, None, weight, bias_ref, taps, copies)


def outer_kernel(
    width, outer, x_ref, low_ref, high_ref, weight, bias_ref, out_ref, taps
):
    def compute(spans):
        return conv_span(width, spans, x_ref, low_ref, high_ref, weight, bias_ref, taps)

    @pl.when(lax.axis_index("frame") == 0)
    def _():
        out_ref[...] = compute(outer)


def convolve_inner(x, taps_weight, bias, width, inner):
    channels = x.shape[1]
    made = sum(count for _, count in inner)
    part = jax.ShapeDtypeStruct((width, channels), jnp.bfloat16)
    return pl.pallas_call(
        functools.partial(inner_kernel, width, inner),
        out_shape=(
            jax.ShapeDtypeStruct((made * width, channels), jnp.bfloat16),
            pltpu.VMEM(x.shape, jnp.bfloat16),
            part,
            part,
            pltpu.VMEM(taps_weight.shape, jnp.bfloat16),
            pltpu.VMEM(bias.shape, jnp.bfloat16),
        ),
        in_specs=[IN_HBM] * 3,
        out_specs=(IN_VMEM,) * 6,
        scratch_shapes=[
            pltpu.VMEM(((made + 2 * len(inner)) * width, 3 * channels), jnp.bfloat16),
            pltpu.SemaphoreType.DMA((5,)),
        ],
        compiler_params=pltpu.CompilerParams(vmem_limit_bytes=CONV_VMEM_BYTES),
        cost_estimate=QUICK,
        name="inner",
    )(*(pltpu.with_memory_space_constraint(each, pltpu.HBM) for each in (x, taps_weight, bias)))


def padded_rows(*many):
    return max(sum(count + 2 for _, count in spans) for spans in many)


def convolve_outer(x, low, high, weight, bias, width, outer):
    channels = x.shape[1]
    made = sum(count for _, count in outer)
    return pl.pallas_call(
        functools.partial(outer_kernel, width, outer),
        out_shape=jax.ShapeDtypeStruct((made * width, channels), jnp.bfloat16),
        in_specs=[IN_VMEM] * 5,
        out_specs=IN_VMEM,
        scratch_shapes=[pltpu.VMEM((padded_rows(outer) * width, 3 * channels), jnp.bfloat16)],
        compiler_params=pltpu.CompilerParams(vmem_limit_bytes=CONV_VMEM_BYTES),
        cost_estimate=QUICK,
        name="outer",
    )(x, low, high, *(pltpu.with_memory_space_constraint(each, pltpu.VMEM) for each in (weight, bias)))


def ask_kernel(
    width, spans, layout, w_query, x_ref, low_ref, high_ref, weight, bias_ref, *refs
):
    pieces, (hidden_ref, queries_ref, taps) = refs[:-3], refs[-3:]

    def lay(values):
        for value, spots in zip(values, layout):
            taken = 0
            for start, size in spots:
                hidden_ref[start : start + size, :] = value[taken : taken + size, :]
                taken += size

    def compute():
        for each, spots in zip(spans, layout):
            lay_one = conv_span(width, each, x_ref, low_ref, high_ref, weight, bias_ref, taps)
            taken = 0
            for start, size in spots:
                hidden_ref[start : start + size, :] = lay_one[taken : taken + size]
                taken += size

    if pieces:
        pl.when(lax.axis_index("frame") == 0)(lambda: lay(pieces))
        pl.when(lax.axis_index("frame") != 0)(compute)
    else:
        compute()
    queries = jnp.dot(hidden_ref[...], w_query[...], preferred_element_type=jnp.float32)
    queries_ref[...] = queries.astype(jnp.bfloat16)


def ask(pieces, x, low, high, weight, bias, w_query, width, spans, layout):
    channels = x.shape[1]
    whole = jax.ShapeDtypeStruct(x.shape, jnp.bfloat16)
    return pl.pallas_call(
        functools.partial(ask_kernel, width, spans, layout),
        out_shape=(whole, whole),
        in_specs=[IN_VMEM] * (len(pieces) + 6),
        out_specs=(IN_VMEM, IN_VMEM),
        scratch_shapes=[pltpu.VMEM((padded_rows(*spans) * width, 3 * channels), jnp.bfloat16)],
        compiler_params=pltpu.CompilerParams(vmem_limit_bytes=CONV_VMEM_BYTES),
        cost_estimate=QUICK,
        name="ask",
    )(w_query, x, low, high, weight, bias, *pieces)


def project_kernel(piece_count, w_keyval, *refs):
    pieces, keyval_ref = refs[:piece_count], refs[piece_count]
    start = 0
    for piece in pieces:
        stop = start + piece.shape[0]
        keyval = jnp.dot(piece[...], w_keyval[...], preferred_element_type=jnp.float32)
        keyval_ref[start:stop, :] = keyval.astype(jnp.bfloat16)
        start = stop


def project(pieces, w_keyval):
    tokens = sum(piece.shape[0] for piece in pieces)
    return pl.pallas_call(
        functools.partial(project_kernel, len(pieces)),
        out_shape=jax.ShapeDtypeStruct((tokens, w_keyval.shape[1]), jnp.bfloat16),
        in_specs=[IN_VMEM] * (len(pieces) + 1),
        out_specs=IN_VMEM,
        compiler_params=pltpu.CompilerParams(vmem_limit_bytes=CONV_VMEM_BYTES),
        cost_estimate=QUICK,
        name="project",
    )(w_keyval, *pieces)


def attend_kernel(part_count, last, queries_ref, keyval, *refs):
    refs = list(refs)
    parts = [[refs.pop(0) for _ in range(3)] for _ in range(part_count)]
    ending = [refs.pop(0) for _ in range(2)] if last else None
    new = [refs.pop(0) for _ in range(1 if last else 3)]
    mixed, joined = refs
    tokens, channels = queries_ref.shape
    key_count = keyval.shape[0]
    all_lanes = [slice(start, start + PAIR) for start in range(0, channels, PAIR)]
    if parts:
        for lanes in all_lanes:
            top = functools.reduce(jnp.maximum, [part[2][:, lanes] for part in parts])
            scales = [jnp.exp(part[2][:, lanes] - top) for part in parts]
            for i in range(2):
                scaled = [part[i][:, lanes] * scale for part, scale in zip(parts, scales)]
                joined[i, :, lanes] = functools.reduce(jnp.add, scaled)
            joined[2, :, lanes] = top
    is_low = lax.broadcasted_iota(jnp.int32, (tokens, PAIR), 1) < HEAD_DIM
    ones = jnp.ones((key_count, PAIR), jnp.bfloat16)

    def scores_of(lanes):
        both = queries_ref[:, lanes] * HEAD_DIM ** (-0.5)
        nothing = jnp.zeros_like(both)
        split = jnp.concatenate(
            [jnp.where(is_low, both, nothing), jnp.where(is_low, nothing, both)], axis=0
        )
        return lax.dot_general(
            split, keyval[:, lanes], (((1,), (1,)), ((), ())), preferred_element_type=jnp.float32
        )

    next_scores = scores_of(all_lanes[0])
    for lanes, next_lanes in zip(all_lanes, all_lanes[1:] + [None]):
        scores = next_scores
        if next_lanes is not None:
            next_scores = scores_of(next_lanes)
        best = jnp.max(scores, axis=1, keepdims=True)
        probability = jnp.exp(scores - best).astype(jnp.bfloat16)
        values = keyval[:, channels + lanes.start : channels + lanes.stop]
        product = jnp.dot(
            probability,
            jnp.concatenate([values, ones], axis=1),
            preferred_element_type=jnp.float32,
        )
        best = jnp.where(is_low, best[:tokens], best[tokens:])
        weighted = jnp.where(is_low, product[:tokens, :PAIR], product[tokens:, :PAIR])
        total = jnp.where(is_low, product[:tokens, PAIR:], product[tokens:, PAIR:])
        if parts:
            top = jnp.maximum(best, joined[2, :, lanes])
            scale, old_scale = jnp.exp(best - top), jnp.exp(joined[2, :, lanes] - top)
            weighted = weighted * scale + joined[0, :, lanes] * old_scale
            total = total * scale + joined[1, :, lanes] * old_scale
        if last:
            mixed[:, lanes] = (weighted / total).astype(jnp.bfloat16)
        else:
            new[0][:, lanes] = weighted
            new[1][:, lanes] = total
            new[2][:, lanes] = best
    if last:
        result = ending[0][...].astype(jnp.float32) + jnp.dot(
            mixed[...], ending[1][...], preferred_element_type=jnp.float32
        )
        new[0][...] = result.astype(jnp.bfloat16)


def attend(queries, keyval, parts, ending, name):
    tokens, channels = queries.shape
    last = ending is not None
    part = jax.ShapeDtypeStruct((tokens, channels), jnp.float32)
    whole = jax.ShapeDtypeStruct((tokens, channels), jnp.bfloat16)
    args = [queries, keyval, *(array for each in parts for array in each), *(ending or ())]
    return pl.pallas_call(
        functools.partial(attend_kernel, len(parts), last),
        out_shape=whole if last else (part,) * 3,
        in_specs=[IN_VMEM] * len(args),
        out_specs=IN_VMEM if last else (IN_VMEM,) * 3,
        scratch_shapes=[
            pltpu.VMEM((tokens, channels), jnp.bfloat16),
            pltpu.VMEM((3, tokens, channels) if parts else (3, 8, PAIR), jnp.float32),
        ],
        compiler_params=pltpu.CompilerParams(vmem_limit_bytes=VMEM_BYTES),
        cost_estimate=QUICK,
        name=name,
    )(*args)


def from_edges(top, bottom):
    count = lax.axis_size("band")
    forward = [(i, i + 1) for i in range(count - 1)]
    backward = [(target, source) for source, target in forward]
    return lax.ppermute(bottom, "band", forward), lax.ppermute(top, "band", backward)


def permute(value, pairs):
    bands = lax.axis_size("band")
    flat = [(source[0] * bands + source[1], target[0] * bands + target[1]) for source, target in pairs]
    return lax.ppermute(value, ("frame", "band"), flat)


def ordered(value, *before):
    return lax.optimization_barrier((value, *before))[0]


def step_across(own, is_source, before=()):
    pairs = [((0, b), (1, b)) for b in range(lax.axis_size("band")) if b % 2]
    if lax.axis_size("frame") == 1:
        return own
    return jnp.where(is_source, own, ordered(permute(own, pairs), *before))


def cast(roots, before=()):
    frames, bands = lax.axis_size("frame"), lax.axis_size("band")
    places = frames // 2
    held, reach = list(roots), places
    while reach > 1:
        reach //= 2
        pairs = [
            ((2 * i + b % 2, b), (2 * (i + reach) + b % 2, b))
            for i in range(0, places, 2 * reach)
            for b in range(bands)
        ]
        arrived = [permute(each, pairs) for each in held]
        if before:
            arrived[0] = ordered(arrived[0], *before)
        held = [have + new for have, new in zip(held, arrived)]
        before = ()
    return held


def exchange(held):
    frames, bands = lax.axis_size("frame"), lax.axis_size("band")
    holders = [(f, b) for f in range(frames) for b in range(bands) if f % 2 == b % 2]
    diagonal = permute(held, [((f, b), (f ^ 1, b ^ 2)) for f, b in holders if f != 1])
    beside = permute(held, [((f, b), (f ^ 1, b)) for f, b in holders if f != 1])
    far = permute(
        held,
        [((f, b), (f, b ^ 2)) for f, b in holders] + [((0, b), (0, b ^ 2)) for b in range(bands) if b % 2],
    )
    return beside, diagonal, far


def swap_cores(value):
    frames, bands = lax.axis_size("frame"), lax.axis_size("band")
    return permute(value, [((f, b), (f, b ^ 1)) for f in range(frames) for b in range(bands)])


def own_side(held, parts):
    beside, diagonal, far = parts
    return [held + beside, far + diagonal]


def sees_all(chunks, starts, early, keyval_of, look):
    frames, bands = lax.axis_size("frame"), lax.axis_size("band")
    if frames < 2 or frames & (frames - 1) or bands != 4:
        return [], keyval_of([lax.all_gather(chunk, ("frame", "band"))[b] for chunk in chunks for b in range(bands)])
    held0, held1 = cast(starts, (*early, starts[1]))
    parts0 = exchange(held0)
    parts0 = (parts0[2], parts0[1], parts0[0])
    held1 = ordered(held1, held0)
    parts1 = exchange(held1)
    parts1 = (parts1[2], parts1[1], parts1[0])
    here0 = keyval_of(own_side(held0, [ordered(parts0, held1)[i] for i in (2, 1, 0)]))
    there0 = swap_cores(here0)
    look0 = look(here0)
    here1 = keyval_of(own_side(held1, [ordered(parts1, look0)[i] for i in (2, 1, 0)]))
    there1 = swap_cores(here1)
    look1 = look(ordered(there0, look0, here1))
    look2 = look(ordered(here1, look1))
    return [look0, look1, look2], ordered(there1, look2)


def per_device(latents, conv_weight, conv_bias, w_query, w_keyval, w_out):
    frames, row_count, width, channels = latents.shape
    tokens = row_count * width
    half = row_count // 2
    taps_weight = conv_weight.reshape(3, 3 * channels, channels)
    inner = ((1, half),)
    outer = ((0, 1), (half + 1, row_count - half - 1))
    seam = (half + 1) * width
    layout = (((0, width), (seam, tokens - seam)), ((width, half * width),))
    latents, is_source = lax.optimization_barrier((latents, lax.axis_index("frame") == 0))
    blocks = [latents[frame].reshape(tokens, channels) for frame in range(frames)]
    first, at_hand, top, bottom, *weight_bias = convolve_inner(
        blocks[0], taps_weight, conv_bias, width, inner
    )
    low, high = from_edges(top, bottom)
    begun = step_across(first, is_source, (low, high))
    second = convolve_outer(at_hand, low, high, *weight_bias, width, outer)
    asked = [
        ask((second, first), at_hand, low, high, taps_weight, conv_bias, w_query, width, (outer, inner), layout)
    ]
    for block in blocks[1:]:
        edges = from_edges(block[:width], block[-width:])
        asked.append(ask((), block, *edges, taps_weight, conv_bias, w_query, width, (outer, inner), layout))
    chunks = (first, second)
    starts = (begun, step_across(second, is_source))

    def keyval_of(pieces):
        return project(pieces, w_keyval)

    def look(keyval):
        return tuple(attend(queries, keyval, (), None, "attend") for _, queries in asked)

    looks, keyval = sees_all(chunks, starts, [queries for _, queries in asked], keyval_of, look)
    results = [
        attend(queries, keyval, [each[i] for each in looks], (hidden, w_out), "join")
        for i, (hidden, queries) in enumerate(asked)
    ]
    return jnp.stack(results).reshape(latents.shape)


def solution(mesh):
    return jax.shard_map(
        per_device,
        mesh=mesh,
        in_specs=(P("frame", "band", None, None), P(), P(), P(), P(), P()),
        out_specs=P("frame", "band", None, None),
        check_vma=False,
    )
```

```python
import functools

import jax
import jax.numpy as jnp
from jax import lax
from jax.experimental import pallas as pl
from jax.experimental.pallas import tpu as pltpu
from jax.sharding import PartitionSpec as P

HEAD_DIM = 64
PAIR = 2 * HEAD_DIM
VMEM_BYTES = 36 * 2**20
CONV_VMEM_BYTES = 28 * 2**20
IN_VMEM = pl.BlockSpec(memory_space=pltpu.VMEM)
IN_PLACE = pl.BlockSpec(memory_space=pl.ANY)
IN_HBM = pl.BlockSpec(memory_space=pltpu.HBM)
SHIFTS = (1, 0, 2)
QUICK = pl.CostEstimate(flops=1, bytes_accessed=1, transcendentals=0)


def conv_span(width, spans, x_ref, low_ref, high_ref, weight, bias_ref, taps, waits=None):
    tokens, channels = x_ref.shape
    last_row = tokens // width
    blocks, starts, place = [], [], 0
    for first, count in spans:
        begin, end = max(first - 1, 0), min(first + count + 1, last_row)
        starts.append(place)
        if first == 0:
            blocks.append(low_ref[...])
        blocks.append(x_ref[begin * width : end * width, :])
        if first + count == last_row:
            blocks.append(high_ref[...])
        place += count + 2
    padded = place * width
    raw = (blocks[0] if len(blocks) == 1 else jnp.concatenate(blocks, axis=0)).astype(jnp.float32)
    active = raw * jax.nn.sigmoid(raw)
    column = lax.rem(lax.broadcasted_iota(jnp.int32, (padded, 1), 0), width)
    before = jnp.where(column == 0, 0.0, pltpu.roll(active, 1, 0))
    after = jnp.where(column == width - 1, 0.0, pltpu.roll(active, padded - 1, 0))
    taps[:padded, :channels] = before.astype(jnp.bfloat16)
    taps[:padded, channels : 2 * channels] = active.astype(jnp.bfloat16)
    taps[:padded, 2 * channels :] = after.astype(jnp.bfloat16)

    def joined(parts):
        return parts[0] if len(parts) == 1 else jnp.concatenate(parts, axis=0)

    own = joined([x_ref[first * width : (first + count) * width, :] for first, count in spans])
    total = own.astype(jnp.float32) + bias_ref[...].astype(jnp.float32)[None, :]
    for shift in SHIFTS:
        if waits:
            waits[shift].wait()
        rows = joined(
            [
                taps[(start + shift) * width : (start + shift + count) * width, :]
                for start, (_, count) in zip(starts, spans)
            ]
        )
        total = total + jnp.dot(rows, weight[shift], preferred_element_type=jnp.float32)
    return total.astype(jnp.bfloat16)


def inner_kernel(
    width, spans, x_hbm, weight_hbm, bias_hbm, out_ref, x_ref, top_ref, bottom_ref, weight, bias_ref, taps, sems
):
    x_copy = pltpu.make_async_copy(x_hbm, x_ref, sems.at[3])
    bias_copy = pltpu.make_async_copy(bias_hbm, bias_ref, sems.at[4])
    copies = [
        pltpu.make_async_copy(weight_hbm.at[shift], weight.at[shift], sems.at[shift])
        for shift in range(3)
    ]
    is_source = lax.axis_index("frame") == 0
    x_copy.start()

    @pl.when(is_source)
    def _():
        bias_copy.start()
        for shift in SHIFTS:
            copies[shift].start()

    x_copy.wait()
    top_ref[...] = x_ref[:width, :]
    bottom_ref[...] = x_ref[x_ref.shape[0] - width :, :]

    @pl.when(is_source)
    def _():
        bias_copy.wait()
        out_ref[...] = conv_span(width, spans, x_ref, None, None, weight, bias_ref, taps, copies)


def outer_kernel(
    width, outer, x_ref, low_ref, high_ref, weight, bias_ref, out_ref, taps
):
    def compute(spans):
        return conv_span(width, spans, x_ref, low_ref, high_ref, weight, bias_ref, taps)

    @pl.when(lax.axis_index("frame") == 0)
    def _():
        out_ref[...] = compute(outer)


def convolve_inner(x, taps_weight, bias, width, inner):
    channels = x.shape[1]
    made = sum(count for _, count in inner)
    part = jax.ShapeDtypeStruct((width, channels), jnp.bfloat16)
    return pl.pallas_call(
        functools.partial(inner_kernel, width, inner),
        out_shape=(
            jax.ShapeDtypeStruct((made * width, channels), jnp.bfloat16),
            pltpu.VMEM(x.shape, jnp.bfloat16),
            part,
            part,
            pltpu.VMEM(taps_weight.shape, jnp.bfloat16),
            pltpu.VMEM(bias.shape, jnp.bfloat16),
        ),
        in_specs=[IN_HBM] * 3,
        out_specs=(IN_VMEM,) * 6,
        scratch_shapes=[
            pltpu.VMEM(((made + 2 * len(inner)) * width, 3 * channels), jnp.bfloat16),
            pltpu.SemaphoreType.DMA((5,)),
        ],
        compiler_params=pltpu.CompilerParams(vmem_limit_bytes=CONV_VMEM_BYTES),
        cost_estimate=QUICK,
        name="inner",
    )(*(pltpu.with_memory_space_constraint(each, pltpu.HBM) for each in (x, taps_weight, bias)))


def padded_rows(*many):
    return max(sum(count + 2 for _, count in spans) for spans in many)


def convolve_outer(x, low, high, weight, bias, width, outer):
    channels = x.shape[1]
    made = sum(count for _, count in outer)
    return pl.pallas_call(
        functools.partial(outer_kernel, width, outer),
        out_shape=jax.ShapeDtypeStruct((made * width, channels), jnp.bfloat16),
        in_specs=[IN_VMEM] * 5,
        out_specs=IN_VMEM,
        scratch_shapes=[pltpu.VMEM((padded_rows(outer) * width, 3 * channels), jnp.bfloat16)],
        compiler_params=pltpu.CompilerParams(vmem_limit_bytes=CONV_VMEM_BYTES),
        cost_estimate=QUICK,
        name="outer",
    )(x, low, high, *(pltpu.with_memory_space_constraint(each, pltpu.VMEM) for each in (weight, bias)))


def ask_kernel(
    width, spans, layout, w_query, x_ref, low_ref, high_ref, weight, bias_ref, *refs
):
    pieces, (hidden_ref, queries_ref, taps) = refs[:-3], refs[-3:]

    def lay(values):
        for value, spots in zip(values, layout):
            taken = 0
            for start, size in spots:
                hidden_ref[start : start + size, :] = value[taken : taken + size, :]
                taken += size

    def compute():
        for each, spots in zip(spans, layout):
            lay_one = conv_span(width, each, x_ref, low_ref, high_ref, weight, bias_ref, taps)
            taken = 0
            for start, size in spots:
                hidden_ref[start : start + size, :] = lay_one[taken : taken + size]
                taken += size

    if pieces:
        pl.when(lax.axis_index("frame") == 0)(lambda: lay(pieces))
        pl.when(lax.axis_index("frame") != 0)(compute)
    else:
        compute()
    queries = jnp.dot(hidden_ref[...], w_query[...], preferred_element_type=jnp.float32)
    queries_ref[...] = queries.astype(jnp.bfloat16)


def ask(pieces, x, low, high, weight, bias, w_query, width, spans, layout):
    channels = x.shape[1]
    whole = jax.ShapeDtypeStruct(x.shape, jnp.bfloat16)
    return pl.pallas_call(
        functools.partial(ask_kernel, width, spans, layout),
        out_shape=(whole, whole),
        in_specs=[IN_VMEM] * (len(pieces) + 6),
        out_specs=(IN_VMEM, IN_VMEM),
        scratch_shapes=[pltpu.VMEM((padded_rows(*spans) * width, 3 * channels), jnp.bfloat16)],
        compiler_params=pltpu.CompilerParams(vmem_limit_bytes=CONV_VMEM_BYTES),
        cost_estimate=QUICK,
        name="ask",
    )(w_query, x, low, high, weight, bias, *pieces)


def project_kernel(piece_count, w_keyval, *refs):
    pieces, keyval_ref = refs[:piece_count], refs[piece_count]
    start = 0
    for piece in pieces:
        stop = start + piece.shape[0]
        keyval = jnp.dot(piece[...], w_keyval[...], preferred_element_type=jnp.float32)
        keyval_ref[start:stop, :] = keyval.astype(jnp.bfloat16)
        start = stop


def project(pieces, w_keyval):
    tokens = sum(piece.shape[0] for piece in pieces)
    return pl.pallas_call(
        functools.partial(project_kernel, len(pieces)),
        out_shape=jax.ShapeDtypeStruct((tokens, w_keyval.shape[1]), jnp.bfloat16),
        in_specs=[IN_VMEM] * (len(pieces) + 1),
        out_specs=IN_VMEM,
        compiler_params=pltpu.CompilerParams(vmem_limit_bytes=CONV_VMEM_BYTES),
        cost_estimate=QUICK,
        name="project",
    )(w_keyval, *pieces)


def attend_kernel(part_count, last, queries_ref, keyval, *refs):
    refs = list(refs)
    parts = [[refs.pop(0) for _ in range(3)] for _ in range(part_count)]
    ending = [refs.pop(0) for _ in range(2)] if last else None
    new = [refs.pop(0) for _ in range(1 if last else 3)]
    mixed, joined = refs
    tokens, channels = queries_ref.shape
    key_count = keyval.shape[0]
    all_lanes = [slice(start, start + PAIR) for start in range(0, channels, PAIR)]
    if parts:
        for lanes in all_lanes:
            top = functools.reduce(jnp.maximum, [part[2][:, lanes] for part in parts])
            scales = [jnp.exp(part[2][:, lanes] - top) for part in parts]
            for i in range(2):
                scaled = [part[i][:, lanes] * scale for part, scale in zip(parts, scales)]
                joined[i, :, lanes] = functools.reduce(jnp.add, scaled)
            joined[2, :, lanes] = top
    is_low = lax.broadcasted_iota(jnp.int32, (tokens, PAIR), 1) < HEAD_DIM
    ones = jnp.ones((key_count, PAIR), jnp.bfloat16)

    def scores_of(lanes):
        both = queries_ref[:, lanes] * HEAD_DIM ** (-0.5)
        nothing = jnp.zeros_like(both)
        split = jnp.concatenate(
            [jnp.where(is_low, both, nothing), jnp.where(is_low, nothing, both)], axis=0
        )
        return lax.dot_general(
            split, keyval[:, lanes], (((1,), (1,)), ((), ())), preferred_element_type=jnp.float32
        )

    next_scores = scores_of(all_lanes[0])
    for lanes, next_lanes in zip(all_lanes, all_lanes[1:] + [None]):
        scores = next_scores
        if next_lanes is not None:
            next_scores = scores_of(next_lanes)
        best = jnp.max(scores, axis=1, keepdims=True)
        probability = jnp.exp(scores - best).astype(jnp.bfloat16)
        values = keyval[:, channels + lanes.start : channels + lanes.stop]
        product = jnp.dot(
            probability,
            jnp.concatenate([values, ones], axis=1),
            preferred_element_type=jnp.float32,
        )
        best = jnp.where(is_low, best[:tokens], best[tokens:])
        weighted = jnp.where(is_low, product[:tokens, :PAIR], product[tokens:, :PAIR])
        total = jnp.where(is_low, product[:tokens, PAIR:], product[tokens:, PAIR:])
        if parts:
            top = jnp.maximum(best, joined[2, :, lanes])
            scale, old_scale = jnp.exp(best - top), jnp.exp(joined[2, :, lanes] - top)
            weighted = weighted * scale + joined[0, :, lanes] * old_scale
            total = total * scale + joined[1, :, lanes] * old_scale
        if last:
            mixed[:, lanes] = (weighted / total).astype(jnp.bfloat16)
        else:
            new[0][:, lanes] = weighted
            new[1][:, lanes] = total
            new[2][:, lanes] = best
    if last:
        result = ending[0][...].astype(jnp.float32) + jnp.dot(
            mixed[...], ending[1][...], preferred_element_type=jnp.float32
        )
        new[0][...] = result.astype(jnp.bfloat16)


def attend(queries, keyval, parts, ending, name):
    tokens, channels = queries.shape
    last = ending is not None
    part = jax.ShapeDtypeStruct((tokens, channels), jnp.float32)
    whole = jax.ShapeDtypeStruct((tokens, channels), jnp.bfloat16)
    args = [queries, keyval, *(array for each in parts for array in each), *(ending or ())]
    return pl.pallas_call(
        functools.partial(attend_kernel, len(parts), last),
        out_shape=whole if last else (part,) * 3,
        in_specs=[IN_VMEM] * len(args),
        out_specs=IN_VMEM if last else (IN_VMEM,) * 3,
        scratch_shapes=[
            pltpu.VMEM((tokens, channels), jnp.bfloat16),
            pltpu.VMEM((3, tokens, channels) if parts else (3, 8, PAIR), jnp.float32),
        ],
        compiler_params=pltpu.CompilerParams(vmem_limit_bytes=VMEM_BYTES),
        cost_estimate=QUICK,
        name=name,
    )(*args)


def from_edges(top, bottom):
    count = lax.axis_size("band")
    forward = [(i, i + 1) for i in range(count - 1)]
    backward = [(target, source) for source, target in forward]
    return lax.ppermute(bottom, "band", forward), lax.ppermute(top, "band", backward)


def permute(value, pairs):
    bands = lax.axis_size("band")
    flat = [(source[0] * bands + source[1], target[0] * bands + target[1]) for source, target in pairs]
    return lax.ppermute(value, ("frame", "band"), flat)


def ordered(value, *before):
    return lax.optimization_barrier((value, *before))[0]


def step_across(own, is_source, before=()):
    pairs = [((0, b), (1, b)) for b in range(lax.axis_size("band")) if b % 2]
    if lax.axis_size("frame") == 1:
        return own
    return jnp.where(is_source, own, ordered(permute(own, pairs), *before))


def cast(roots, before=()):
    frames, bands = lax.axis_size("frame"), lax.axis_size("band")
    places = frames // 2
    held, reach = list(roots), places
    while reach > 1:
        reach //= 2
        pairs = [
            ((2 * i + b % 2, b), (2 * (i + reach) + b % 2, b))
            for i in range(0, places, 2 * reach)
            for b in range(bands)
        ]
        arrived = [permute(each, pairs) for each in held]
        if before:
            arrived[0] = ordered(arrived[0], *before)
        held = [have + new for have, new in zip(held, arrived)]
        before = ()
    return held


def exchange(held):
    frames, bands = lax.axis_size("frame"), lax.axis_size("band")
    holders = [(f, b) for f in range(frames) for b in range(bands) if f % 2 == b % 2]
    diagonal = permute(held, [((f, b), (f ^ 1, b ^ 2)) for f, b in holders if f != 1])
    beside = permute(held, [((f, b), (f ^ 1, b)) for f, b in holders if f != 1])
    far = permute(
        held,
        [((f, b), (f, b ^ 2)) for f, b in holders] + [((0, b), (0, b ^ 2)) for b in range(bands) if b % 2],
    )
    return beside, diagonal, far


def swap_cores(value):
    frames, bands = lax.axis_size("frame"), lax.axis_size("band")
    return permute(value, [((f, b), (f, b ^ 1)) for f in range(frames) for b in range(bands)])


def own_side(held, parts):
    beside, diagonal, far = parts
    return [held + beside, far + diagonal]


def sees_all(chunks, starts, early, keyval_of, look):
    frames, bands = lax.axis_size("frame"), lax.axis_size("band")
    if frames < 2 or frames & (frames - 1) or bands != 4:
        return [], keyval_of([lax.all_gather(chunk, ("frame", "band"))[b] for chunk in chunks for b in range(bands)])
    held0, held1 = cast(starts, (*early, starts[1]))
    parts0 = exchange(held0)
    parts0 = (parts0[2], parts0[1], parts0[0])
    held1 = ordered(held1, held0)
    parts1 = exchange(held1)
    parts1 = (parts1[1], parts1[2], parts1[0])
    here0 = keyval_of(own_side(held0, [ordered(parts0, held1)[i] for i in (2, 1, 0)]))
    there0 = swap_cores(here0)
    look0 = look(here0)
    here1 = keyval_of(own_side(held1, [ordered(parts1, look0)[i] for i in (2, 0, 1)]))
    there1 = swap_cores(here1)
    look1 = look(ordered(there0, look0, here1))
    look2 = look(ordered(here1, look1))
    return [look0, look1, look2], ordered(there1, look2)


def per_device(latents, conv_weight, conv_bias, w_query, w_keyval, w_out):
    frames, row_count, width, channels = latents.shape
    tokens = row_count * width
    half = row_count // 2
    taps_weight = conv_weight.reshape(3, 3 * channels, channels)
    inner = ((1, half),)
    outer = ((0, 1), (half + 1, row_count - half - 1))
    seam = (half + 1) * width
    layout = (((0, width), (seam, tokens - seam)), ((width, half * width),))
    latents, is_source = lax.optimization_barrier((latents, lax.axis_index("frame") == 0))
    blocks = [latents[frame].reshape(tokens, channels) for frame in range(frames)]
    first, at_hand, top, bottom, *weight_bias = convolve_inner(
        blocks[0], taps_weight, conv_bias, width, inner
    )
    low, high = from_edges(top, bottom)
    begun = step_across(first, is_source, (low, high))
    second = convolve_outer(at_hand, low, high, *weight_bias, width, outer)
    asked = [
        ask((second, first), at_hand, low, high, taps_weight, conv_bias, w_query, width, (outer, inner), layout)
    ]
    for block in blocks[1:]:
        edges = from_edges(block[:width], block[-width:])
        asked.append(ask((), block, *edges, taps_weight, conv_bias, w_query, width, (outer, inner), layout))
    chunks = (first, second)
    starts = (begun, step_across(second, is_source))

    def keyval_of(pieces):
        return project(pieces, w_keyval)

    def look(keyval):
        return tuple(attend(queries, keyval, (), None, "attend") for _, queries in asked)

    looks, keyval = sees_all(chunks, starts, [queries for _, queries in asked], keyval_of, look)
    results = [
        attend(queries, keyval, [each[i] for each in looks], (hidden, w_out), "join")
        for i, (hidden, queries) in enumerate(asked)
    ]
    return jnp.stack(results).reshape(latents.shape)


def solution(mesh):
    return jax.shard_map(
        per_device,
        mesh=mesh,
        in_specs=(P("frame", "band", None, None), P(), P(), P(), P(), P()),
        out_specs=P("frame", "band", None, None),
        check_vma=False,
    )
```

```python
import functools

import jax
import jax.numpy as jnp
from jax import lax
from jax.experimental import pallas as pl
from jax.experimental.pallas import tpu as pltpu
from jax.sharding import PartitionSpec as P

HEAD_DIM = 64
PAIR = 2 * HEAD_DIM
VMEM_BYTES = 36 * 2**20
CONV_VMEM_BYTES = 28 * 2**20
IN_VMEM = pl.BlockSpec(memory_space=pltpu.VMEM)
IN_PLACE = pl.BlockSpec(memory_space=pl.ANY)
IN_HBM = pl.BlockSpec(memory_space=pltpu.HBM)
SHIFTS = (1, 0, 2)
QUICK = pl.CostEstimate(flops=1, bytes_accessed=1, transcendentals=0)


def conv_span(width, spans, x_ref, low_ref, high_ref, weight, bias_ref, taps, waits=None):
    tokens, channels = x_ref.shape
    last_row = tokens // width
    blocks, starts, place = [], [], 0
    for first, count in spans:
        begin, end = max(first - 1, 0), min(first + count + 1, last_row)
        starts.append(place)
        if first == 0:
            blocks.append(low_ref[...])
        blocks.append(x_ref[begin * width : end * width, :])
        if first + count == last_row:
            blocks.append(high_ref[...])
        place += count + 2
    padded = place * width
    raw = (blocks[0] if len(blocks) == 1 else jnp.concatenate(blocks, axis=0)).astype(jnp.float32)
    active = raw * jax.nn.sigmoid(raw)
    column = lax.rem(lax.broadcasted_iota(jnp.int32, (padded, 1), 0), width)
    before = jnp.where(column == 0, 0.0, pltpu.roll(active, 1, 0))
    after = jnp.where(column == width - 1, 0.0, pltpu.roll(active, padded - 1, 0))
    taps[:padded, :channels] = before.astype(jnp.bfloat16)
    taps[:padded, channels : 2 * channels] = active.astype(jnp.bfloat16)
    taps[:padded, 2 * channels :] = after.astype(jnp.bfloat16)

    def joined(parts):
        return parts[0] if len(parts) == 1 else jnp.concatenate(parts, axis=0)

    own = joined([x_ref[first * width : (first + count) * width, :] for first, count in spans])
    total = own.astype(jnp.float32) + bias_ref[...].astype(jnp.float32)[None, :]
    for shift in SHIFTS:
        if waits:
            waits[shift].wait()
        rows = joined(
            [
                taps[(start + shift) * width : (start + shift + count) * width, :]
                for start, (_, count) in zip(starts, spans)
            ]
        )
        total = total + jnp.dot(rows, weight[shift], preferred_element_type=jnp.float32)
    return total.astype(jnp.bfloat16)


def inner_kernel(
    width, spans, x_hbm, weight_hbm, bias_hbm, out_ref, x_ref, top_ref, bottom_ref, weight, bias_ref, taps, sems
):
    x_copy = pltpu.make_async_copy(x_hbm, x_ref, sems.at[3])
    bias_copy = pltpu.make_async_copy(bias_hbm, bias_ref, sems.at[4])
    copies = [
        pltpu.make_async_copy(weight_hbm.at[shift], weight.at[shift], sems.at[shift])
        for shift in range(3)
    ]
    is_source = lax.axis_index("frame") == 0
    x_copy.start()

    @pl.when(is_source)
    def _():
        bias_copy.start()
        for shift in SHIFTS:
            copies[shift].start()

    x_copy.wait()
    top_ref[...] = x_ref[:width, :]
    bottom_ref[...] = x_ref[x_ref.shape[0] - width :, :]

    @pl.when(is_source)
    def _():
        bias_copy.wait()
        out_ref[...] = conv_span(width, spans, x_ref, None, None, weight, bias_ref, taps, copies)


def outer_kernel(
    width, outer, x_ref, low_ref, high_ref, weight, bias_ref, out_ref, taps
):
    def compute(spans):
        return conv_span(width, spans, x_ref, low_ref, high_ref, weight, bias_ref, taps)

    @pl.when(lax.axis_index("frame") == 0)
    def _():
        out_ref[...] = compute(outer)


def convolve_inner(x, taps_weight, bias, width, inner):
    channels = x.shape[1]
    made = sum(count for _, count in inner)
    part = jax.ShapeDtypeStruct((width, channels), jnp.bfloat16)
    return pl.pallas_call(
        functools.partial(inner_kernel, width, inner),
        out_shape=(
            jax.ShapeDtypeStruct((made * width, channels), jnp.bfloat16),
            pltpu.VMEM(x.shape, jnp.bfloat16),
            part,
            part,
            pltpu.VMEM(taps_weight.shape, jnp.bfloat16),
            pltpu.VMEM(bias.shape, jnp.bfloat16),
        ),
        in_specs=[IN_HBM] * 3,
        out_specs=(IN_VMEM,) * 6,
        scratch_shapes=[
            pltpu.VMEM(((made + 2 * len(inner)) * width, 3 * channels), jnp.bfloat16),
            pltpu.SemaphoreType.DMA((5,)),
        ],
        compiler_params=pltpu.CompilerParams(vmem_limit_bytes=CONV_VMEM_BYTES),
        cost_estimate=QUICK,
        name="inner",
    )(*(pltpu.with_memory_space_constraint(each, pltpu.HBM) for each in (x, taps_weight, bias)))


def padded_rows(*many):
    return max(sum(count + 2 for _, count in spans) for spans in many)


def convolve_outer(x, low, high, weight, bias, width, outer):
    channels = x.shape[1]
    made = sum(count for _, count in outer)
    return pl.pallas_call(
        functools.partial(outer_kernel, width, outer),
        out_shape=jax.ShapeDtypeStruct((made * width, channels), jnp.bfloat16),
        in_specs=[IN_VMEM] * 5,
        out_specs=IN_VMEM,
        scratch_shapes=[pltpu.VMEM((padded_rows(outer) * width, 3 * channels), jnp.bfloat16)],
        compiler_params=pltpu.CompilerParams(vmem_limit_bytes=CONV_VMEM_BYTES),
        cost_estimate=QUICK,
        name="outer",
    )(x, low, high, *(pltpu.with_memory_space_constraint(each, pltpu.VMEM) for each in (weight, bias)))


def ask_kernel(
    width, spans, layout, w_query, x_ref, low_ref, high_ref, weight, bias_ref, *refs
):
    pieces, (hidden_ref, queries_ref, taps) = refs[:-3], refs[-3:]

    def lay(values):
        for value, spots in zip(values, layout):
            taken = 0
            for start, size in spots:
                hidden_ref[start : start + size, :] = value[taken : taken + size, :]
                taken += size

    def compute():
        for each, spots in zip(spans, layout):
            lay_one = conv_span(width, each, x_ref, low_ref, high_ref, weight, bias_ref, taps)
            taken = 0
            for start, size in spots:
                hidden_ref[start : start + size, :] = lay_one[taken : taken + size]
                taken += size

    if pieces:
        pl.when(lax.axis_index("frame") == 0)(lambda: lay(pieces))
        pl.when(lax.axis_index("frame") != 0)(compute)
    else:
        compute()
    queries = jnp.dot(hidden_ref[...], w_query[...], preferred_element_type=jnp.float32)
    queries_ref[...] = queries.astype(jnp.bfloat16)


def ask(pieces, x, low, high, weight, bias, w_query, width, spans, layout):
    channels = x.shape[1]
    whole = jax.ShapeDtypeStruct(x.shape, jnp.bfloat16)
    return pl.pallas_call(
        functools.partial(ask_kernel, width, spans, layout),
        out_shape=(whole, whole),
        in_specs=[IN_VMEM] * (len(pieces) + 6),
        out_specs=(IN_VMEM, IN_VMEM),
        scratch_shapes=[pltpu.VMEM((padded_rows(*spans) * width, 3 * channels), jnp.bfloat16)],
        compiler_params=pltpu.CompilerParams(vmem_limit_bytes=CONV_VMEM_BYTES),
        cost_estimate=QUICK,
        name="ask",
    )(w_query, x, low, high, weight, bias, *pieces)


def project_kernel(w_keyval, *refs):
    halves, keyval_ref = refs[:-1], refs[-1]
    start = 0
    for one, other in zip(halves[::2], halves[1::2]):
        stop = start + one.shape[0]
        piece = one[...] + other[...]
        keyval = jnp.dot(piece, w_keyval[...], preferred_element_type=jnp.float32)
        keyval_ref[start:stop, :] = keyval.astype(jnp.bfloat16)
        start = stop


def project(pieces, w_keyval):
    tokens = sum(one.shape[0] for one, _ in pieces)
    return pl.pallas_call(
        project_kernel,
        out_shape=jax.ShapeDtypeStruct((tokens, w_keyval.shape[1]), jnp.bfloat16),
        in_specs=[IN_VMEM] * (2 * len(pieces) + 1),
        out_specs=IN_VMEM,
        compiler_params=pltpu.CompilerParams(vmem_limit_bytes=CONV_VMEM_BYTES),
        cost_estimate=QUICK,
        name="project",
    )(w_keyval, *(half for piece in pieces for half in piece))


def attend_kernel(part_count, last, queries_ref, keyval, *refs):
    refs = list(refs)
    parts = [[refs.pop(0) for _ in range(3)] for _ in range(part_count)]
    ending = [refs.pop(0) for _ in range(2)] if last else None
    new = [refs.pop(0) for _ in range(1 if last else 3)]
    mixed, joined = refs
    tokens, channels = queries_ref.shape
    key_count = keyval.shape[0]
    all_lanes = [slice(start, start + PAIR) for start in range(0, channels, PAIR)]
    if parts:
        for lanes in all_lanes:
            top = functools.reduce(jnp.maximum, [part[2][:, lanes] for part in parts])
            scales = [jnp.exp(part[2][:, lanes] - top) for part in parts]
            for i in range(2):
                scaled = [part[i][:, lanes] * scale for part, scale in zip(parts, scales)]
                joined[i, :, lanes] = functools.reduce(jnp.add, scaled)
            joined[2, :, lanes] = top
    is_low = lax.broadcasted_iota(jnp.int32, (tokens, PAIR), 1) < HEAD_DIM
    ones = jnp.ones((key_count, PAIR), jnp.bfloat16)

    def scores_of(lanes):
        both = queries_ref[:, lanes] * HEAD_DIM ** (-0.5)
        nothing = jnp.zeros_like(both)
        split = jnp.concatenate(
            [jnp.where(is_low, both, nothing), jnp.where(is_low, nothing, both)], axis=0
        )
        return lax.dot_general(
            split, keyval[:, lanes], (((1,), (1,)), ((), ())), preferred_element_type=jnp.float32
        )

    next_scores = scores_of(all_lanes[0])
    for lanes, next_lanes in zip(all_lanes, all_lanes[1:] + [None]):
        scores = next_scores
        if next_lanes is not None:
            next_scores = scores_of(next_lanes)
        best = jnp.max(scores, axis=1, keepdims=True)
        probability = jnp.exp(scores - best).astype(jnp.bfloat16)
        values = keyval[:, channels + lanes.start : channels + lanes.stop]
        product = jnp.dot(
            probability,
            jnp.concatenate([values, ones], axis=1),
            preferred_element_type=jnp.float32,
        )
        best = jnp.where(is_low, best[:tokens], best[tokens:])
        weighted = jnp.where(is_low, product[:tokens, :PAIR], product[tokens:, :PAIR])
        total = jnp.where(is_low, product[:tokens, PAIR:], product[tokens:, PAIR:])
        if parts:
            top = jnp.maximum(best, joined[2, :, lanes])
            scale, old_scale = jnp.exp(best - top), jnp.exp(joined[2, :, lanes] - top)
            weighted = weighted * scale + joined[0, :, lanes] * old_scale
            total = total * scale + joined[1, :, lanes] * old_scale
        if last:
            mixed[:, lanes] = (weighted / total).astype(jnp.bfloat16)
        else:
            new[0][:, lanes] = weighted
            new[1][:, lanes] = total
            new[2][:, lanes] = best
    if last:
        result = ending[0][...].astype(jnp.float32) + jnp.dot(
            mixed[...], ending[1][...], preferred_element_type=jnp.float32
        )
        new[0][...] = result.astype(jnp.bfloat16)


def attend(queries, keyval, parts, ending, name):
    tokens, channels = queries.shape
    last = ending is not None
    part = jax.ShapeDtypeStruct((tokens, channels), jnp.float32)
    whole = jax.ShapeDtypeStruct((tokens, channels), jnp.bfloat16)
    args = [queries, keyval, *(array for each in parts for array in each), *(ending or ())]
    return pl.pallas_call(
        functools.partial(attend_kernel, len(parts), last),
        out_shape=whole if last else (part,) * 3,
        in_specs=[IN_VMEM] * len(args),
        out_specs=IN_VMEM if last else (IN_VMEM,) * 3,
        scratch_shapes=[
            pltpu.VMEM((tokens, channels), jnp.bfloat16),
            pltpu.VMEM((3, tokens, channels) if parts else (3, 8, PAIR), jnp.float32),
        ],
        compiler_params=pltpu.CompilerParams(vmem_limit_bytes=VMEM_BYTES),
        cost_estimate=QUICK,
        name=name,
    )(*args)


def from_edges(top, bottom):
    count = lax.axis_size("band")
    forward = [(i, i + 1) for i in range(count - 1)]
    backward = [(target, source) for source, target in forward]
    return lax.ppermute(bottom, "band", forward), lax.ppermute(top, "band", backward)


def permute(value, pairs):
    bands = lax.axis_size("band")
    flat = [(source[0] * bands + source[1], target[0] * bands + target[1]) for source, target in pairs]
    return lax.ppermute(value, ("frame", "band"), flat)


def ordered(value, *before):
    return lax.optimization_barrier((value, *before))[0]


def step_across(own, is_source, before=()):
    pairs = [((0, b), (1, b)) for b in range(lax.axis_size("band")) if b % 2]
    if lax.axis_size("frame") == 1:
        return own
    return jnp.where(is_source, own, ordered(permute(own, pairs), *before))


def cast(roots, before=()):
    frames, bands = lax.axis_size("frame"), lax.axis_size("band")
    places = frames // 2
    held, reach = list(roots), places
    while reach > 1:
        reach //= 2
        pairs = [
            ((2 * i + b % 2, b), (2 * (i + reach) + b % 2, b))
            for i in range(0, places, 2 * reach)
            for b in range(bands)
        ]
        arrived = [permute(each, pairs) for each in held]
        if before:
            arrived[0] = ordered(arrived[0], *before)
        held = [have + new for have, new in zip(held, arrived)]
        before = ()
    return held


def exchange(held):
    frames, bands = lax.axis_size("frame"), lax.axis_size("band")
    holders = [(f, b) for f in range(frames) for b in range(bands) if f % 2 == b % 2]
    diagonal = permute(held, [((f, b), (f ^ 1, b ^ 2)) for f, b in holders if f != 1])
    beside = permute(held, [((f, b), (f ^ 1, b)) for f, b in holders if f != 1])
    far = permute(
        held,
        [((f, b), (f, b ^ 2)) for f, b in holders] + [((0, b), (0, b ^ 2)) for b in range(bands) if b % 2],
    )
    return beside, diagonal, far


def swap_cores(value):
    frames, bands = lax.axis_size("frame"), lax.axis_size("band")
    return permute(value, [((f, b), (f, b ^ 1)) for f in range(frames) for b in range(bands)])


def own_side(held, parts):
    beside, diagonal, far = parts
    return [(held, beside), (far, diagonal)]


def sees_all(chunks, starts, early, keyval_of, look):
    frames, bands = lax.axis_size("frame"), lax.axis_size("band")
    if frames < 2 or frames & (frames - 1) or bands != 4:
        pieces = [lax.all_gather(chunk, ("frame", "band"))[b] for chunk in chunks for b in range(bands)]
        return [], keyval_of([(piece, jnp.zeros_like(piece)) for piece in pieces])
    held0, held1 = cast(starts, (*early, starts[1]))
    parts0 = exchange(held0)
    parts0 = (parts0[2], parts0[1], parts0[0])
    held1 = ordered(held1, held0)
    parts1 = exchange(held1)
    parts1 = (parts1[1], parts1[2], parts1[0])
    here0 = keyval_of(own_side(held0, [ordered(parts0, held1)[i] for i in (2, 1, 0)]))
    there0 = swap_cores(here0)
    look0 = look(here0)
    here1 = keyval_of(own_side(held1, [ordered(parts1, look0)[i] for i in (2, 0, 1)]))
    there1 = swap_cores(here1)
    look1 = look(ordered(there0, look0, here1))
    look2 = look(ordered(here1, look1))
    return [look0, look1, look2], ordered(there1, look2)


def per_device(latents, conv_weight, conv_bias, w_query, w_keyval, w_out):
    frames, row_count, width, channels = latents.shape
    tokens = row_count * width
    half = row_count // 2
    taps_weight = conv_weight.reshape(3, 3 * channels, channels)
    inner = ((1, half),)
    outer = ((0, 1), (half + 1, row_count - half - 1))
    seam = (half + 1) * width
    layout = (((0, width), (seam, tokens - seam)), ((width, half * width),))
    latents, is_source = lax.optimization_barrier((latents, lax.axis_index("frame") == 0))
    blocks = [latents[frame].reshape(tokens, channels) for frame in range(frames)]
    first, at_hand, top, bottom, *weight_bias = convolve_inner(
        blocks[0], taps_weight, conv_bias, width, inner
    )
    low, high = from_edges(top, bottom)
    begun = step_across(first, is_source, (low, high))
    second = convolve_outer(at_hand, low, high, *weight_bias, width, outer)
    asked = [
        ask((second, first), at_hand, low, high, taps_weight, conv_bias, w_query, width, (outer, inner), layout)
    ]
    for block in blocks[1:]:
        edges = from_edges(block[:width], block[-width:])
        asked.append(ask((), block, *edges, taps_weight, conv_bias, w_query, width, (outer, inner), layout))
    chunks = (first, second)
    starts = (begun, step_across(second, is_source))

    def keyval_of(pieces):
        return project(pieces, w_keyval)

    def look(keyval):
        return tuple(attend(queries, keyval, (), None, "attend") for _, queries in asked)

    looks, keyval = sees_all(chunks, starts, [queries for _, queries in asked], keyval_of, look)
    results = [
        attend(queries, keyval, [each[i] for each in looks], (hidden, w_out), "join")
        for i, (hidden, queries) in enumerate(asked)
    ]
    return jnp.stack(results).reshape(latents.shape)


def solution(mesh):
    return jax.shard_map(
        per_device,
        mesh=mesh,
        in_specs=(P("frame", "band", None, None), P(), P(), P(), P(), P()),
        out_specs=P("frame", "band", None, None),
        check_vma=False,
    )
```

```python
import functools

import jax
import jax.numpy as jnp
from jax import lax
from jax.experimental import pallas as pl
from jax.experimental.pallas import tpu as pltpu
from jax.sharding import PartitionSpec as P

HEAD_DIM = 64
PAIR = 2 * HEAD_DIM
VMEM_BYTES = 36 * 2**20
CONV_VMEM_BYTES = 28 * 2**20
IN_VMEM = pl.BlockSpec(memory_space=pltpu.VMEM)
IN_PLACE = pl.BlockSpec(memory_space=pl.ANY)
IN_HBM = pl.BlockSpec(memory_space=pltpu.HBM)
SHIFTS = (1, 0, 2)
QUICK = pl.CostEstimate(flops=1, bytes_accessed=1, transcendentals=0)


def conv_span(width, spans, x_ref, low_ref, high_ref, weight, bias_ref, taps, waits=None):
    tokens, channels = x_ref.shape
    last_row = tokens // width
    blocks, starts, place = [], [], 0
    for first, count in spans:
        begin, end = max(first - 1, 0), min(first + count + 1, last_row)
        starts.append(place)
        if first == 0:
            blocks.append(low_ref[...])
        blocks.append(x_ref[begin * width : end * width, :])
        if first + count == last_row:
            blocks.append(high_ref[...])
        place += count + 2
    padded = place * width
    raw = (blocks[0] if len(blocks) == 1 else jnp.concatenate(blocks, axis=0)).astype(jnp.float32)
    active = raw * jax.nn.sigmoid(raw)
    column = lax.rem(lax.broadcasted_iota(jnp.int32, (padded, 1), 0), width)
    before = jnp.where(column == 0, 0.0, pltpu.roll(active, 1, 0))
    after = jnp.where(column == width - 1, 0.0, pltpu.roll(active, padded - 1, 0))
    taps[:padded, :channels] = before.astype(jnp.bfloat16)
    taps[:padded, channels : 2 * channels] = active.astype(jnp.bfloat16)
    taps[:padded, 2 * channels :] = after.astype(jnp.bfloat16)

    def joined(parts):
        return parts[0] if len(parts) == 1 else jnp.concatenate(parts, axis=0)

    own = joined([x_ref[first * width : (first + count) * width, :] for first, count in spans])
    total = own.astype(jnp.float32) + bias_ref[...].astype(jnp.float32)[None, :]
    for shift in SHIFTS:
        if waits:
            waits[shift].wait()
        rows = joined(
            [
                taps[(start + shift) * width : (start + shift + count) * width, :]
                for start, (_, count) in zip(starts, spans)
            ]
        )
        total = total + jnp.dot(rows, weight[shift], preferred_element_type=jnp.float32)
    return total.astype(jnp.bfloat16)


def inner_kernel(
    width, spans, x_hbm, weight_hbm, bias_hbm, out_ref, x_ref, top_ref, bottom_ref, weight, bias_ref, taps, sems
):
    x_copy = pltpu.make_async_copy(x_hbm, x_ref, sems.at[3])
    bias_copy = pltpu.make_async_copy(bias_hbm, bias_ref, sems.at[4])
    copies = [
        pltpu.make_async_copy(weight_hbm.at[shift], weight.at[shift], sems.at[shift])
        for shift in range(3)
    ]
    is_source = lax.axis_index("frame") == 0
    x_copy.start()

    @pl.when(is_source)
    def _():
        bias_copy.start()
        for shift in SHIFTS:
            copies[shift].start()

    x_copy.wait()
    top_ref[...] = x_ref[:width, :]
    bottom_ref[...] = x_ref[x_ref.shape[0] - width :, :]

    @pl.when(is_source)
    def _():
        bias_copy.wait()
        out_ref[...] = conv_span(width, spans, x_ref, None, None, weight, bias_ref, taps, copies)


def outer_kernel(
    width, outer, x_ref, low_ref, high_ref, weight, bias_ref, out_ref, taps
):
    def compute(spans):
        return conv_span(width, spans, x_ref, low_ref, high_ref, weight, bias_ref, taps)

    @pl.when(lax.axis_index("frame") == 0)
    def _():
        out_ref[...] = compute(outer)


def convolve_inner(x, taps_weight, bias, width, inner):
    channels = x.shape[1]
    made = sum(count for _, count in inner)
    part = jax.ShapeDtypeStruct((width, channels), jnp.bfloat16)
    return pl.pallas_call(
        functools.partial(inner_kernel, width, inner),
        out_shape=(
            jax.ShapeDtypeStruct((made * width, channels), jnp.bfloat16),
            pltpu.VMEM(x.shape, jnp.bfloat16),
            part,
            part,
            pltpu.VMEM(taps_weight.shape, jnp.bfloat16),
            pltpu.VMEM(bias.shape, jnp.bfloat16),
        ),
        in_specs=[IN_HBM] * 3,
        out_specs=(IN_VMEM,) * 6,
        scratch_shapes=[
            pltpu.VMEM(((made + 2 * len(inner)) * width, 3 * channels), jnp.bfloat16),
            pltpu.SemaphoreType.DMA((5,)),
        ],
        compiler_params=pltpu.CompilerParams(vmem_limit_bytes=CONV_VMEM_BYTES),
        cost_estimate=QUICK,
        name="inner",
    )(*(pltpu.with_memory_space_constraint(each, pltpu.HBM) for each in (x, taps_weight, bias)))


def padded_rows(*many):
    return max(sum(count + 2 for _, count in spans) for spans in many)


def convolve_outer(x, low, high, weight, bias, width, outer):
    channels = x.shape[1]
    made = sum(count for _, count in outer)
    return pl.pallas_call(
        functools.partial(outer_kernel, width, outer),
        out_shape=jax.ShapeDtypeStruct((made * width, channels), jnp.bfloat16),
        in_specs=[IN_VMEM] * 5,
        out_specs=IN_VMEM,
        scratch_shapes=[pltpu.VMEM((padded_rows(outer) * width, 3 * channels), jnp.bfloat16)],
        compiler_params=pltpu.CompilerParams(vmem_limit_bytes=CONV_VMEM_BYTES),
        cost_estimate=QUICK,
        name="outer",
    )(x, low, high, *(pltpu.with_memory_space_constraint(each, pltpu.VMEM) for each in (weight, bias)))


def ask_kernel(
    width, spans, layout, w_query, x_ref, low_ref, high_ref, weight, bias_ref, *refs
):
    pieces, (hidden_ref, queries_ref, taps) = refs[:-3], refs[-3:]

    def lay(values):
        for value, spots in zip(values, layout):
            taken = 0
            for start, size in spots:
                hidden_ref[start : start + size, :] = value[taken : taken + size, :]
                taken += size

    def compute():
        for each, spots in zip(spans, layout):
            lay_one = conv_span(width, each, x_ref, low_ref, high_ref, weight, bias_ref, taps)
            taken = 0
            for start, size in spots:
                hidden_ref[start : start + size, :] = lay_one[taken : taken + size]
                taken += size

    if pieces:
        pl.when(lax.axis_index("frame") == 0)(lambda: lay(pieces))
        pl.when(lax.axis_index("frame") != 0)(compute)
    else:
        compute()
    queries = jnp.dot(hidden_ref[...], w_query[...], preferred_element_type=jnp.float32)
    queries_ref[...] = queries.astype(jnp.bfloat16)


def ask(pieces, x, low, high, weight, bias, w_query, width, spans, layout):
    channels = x.shape[1]
    whole = jax.ShapeDtypeStruct(x.shape, jnp.bfloat16)
    return pl.pallas_call(
        functools.partial(ask_kernel, width, spans, layout),
        out_shape=(whole, whole),
        in_specs=[IN_VMEM] * (len(pieces) + 6),
        out_specs=(IN_VMEM, IN_VMEM),
        scratch_shapes=[pltpu.VMEM((padded_rows(*spans) * width, 3 * channels), jnp.bfloat16)],
        compiler_params=pltpu.CompilerParams(vmem_limit_bytes=CONV_VMEM_BYTES),
        cost_estimate=QUICK,
        name="ask",
    )(w_query, x, low, high, weight, bias, *pieces)


def project_kernel(piece_count, w_keyval, *refs):
    pieces, keyval_ref = refs[:piece_count], refs[piece_count]
    start = 0
    for piece in pieces:
        stop = start + piece.shape[0]
        keyval = jnp.dot(piece[...], w_keyval[...], preferred_element_type=jnp.float32)
        keyval_ref[start:stop, :] = keyval.astype(jnp.bfloat16)
        start = stop


def project(pieces, w_keyval):
    tokens = sum(piece.shape[0] for piece in pieces)
    return pl.pallas_call(
        functools.partial(project_kernel, len(pieces)),
        out_shape=jax.ShapeDtypeStruct((tokens, w_keyval.shape[1]), jnp.bfloat16),
        in_specs=[IN_VMEM] * (len(pieces) + 1),
        out_specs=IN_VMEM,
        compiler_params=pltpu.CompilerParams(vmem_limit_bytes=CONV_VMEM_BYTES),
        cost_estimate=QUICK,
        name="project",
    )(w_keyval, *pieces)


def attend_kernel(part_count, last, queries_ref, keyval, *refs):
    refs = list(refs)
    parts = [[refs.pop(0) for _ in range(3)] for _ in range(part_count)]
    ending = [refs.pop(0) for _ in range(2)] if last else None
    new = [refs.pop(0) for _ in range(1 if last else 3)]
    mixed, joined = refs
    tokens, channels = queries_ref.shape
    key_count = keyval.shape[0]
    all_lanes = [slice(start, start + PAIR) for start in range(0, channels, PAIR)]
    if parts:
        for lanes in all_lanes:
            top = functools.reduce(jnp.maximum, [part[2][:, lanes] for part in parts])
            scales = [jnp.exp(part[2][:, lanes] - top) for part in parts]
            for i in range(2):
                scaled = [part[i][:, lanes] * scale for part, scale in zip(parts, scales)]
                joined[i, :, lanes] = functools.reduce(jnp.add, scaled)
            joined[2, :, lanes] = top
    is_low = lax.broadcasted_iota(jnp.int32, (tokens, PAIR), 1) < HEAD_DIM
    ones = jnp.ones((key_count, PAIR), jnp.bfloat16)

    def scores_of(lanes):
        both = queries_ref[:, lanes] * HEAD_DIM ** (-0.5)
        nothing = jnp.zeros_like(both)
        split = jnp.concatenate(
            [jnp.where(is_low, both, nothing), jnp.where(is_low, nothing, both)], axis=0
        )
        return lax.dot_general(
            split, keyval[:, lanes], (((1,), (1,)), ((), ())), preferred_element_type=jnp.float32
        )

    next_scores = scores_of(all_lanes[0])
    for lanes, next_lanes in zip(all_lanes, all_lanes[1:] + [None]):
        scores = next_scores
        if next_lanes is not None:
            next_scores = scores_of(next_lanes)
        best = jnp.max(scores, axis=1, keepdims=True)
        probability = jnp.exp(scores - best).astype(jnp.bfloat16)
        values = keyval[:, channels + lanes.start : channels + lanes.stop]
        product = jnp.dot(
            probability,
            jnp.concatenate([values, ones], axis=1),
            preferred_element_type=jnp.float32,
        )
        best = jnp.where(is_low, best[:tokens], best[tokens:])
        weighted = jnp.where(is_low, product[:tokens, :PAIR], product[tokens:, :PAIR])
        total = jnp.where(is_low, product[:tokens, PAIR:], product[tokens:, PAIR:])
        if parts:
            top = jnp.maximum(best, joined[2, :, lanes])
            scale, old_scale = jnp.exp(best - top), jnp.exp(joined[2, :, lanes] - top)
            weighted = weighted * scale + joined[0, :, lanes] * old_scale
            total = total * scale + joined[1, :, lanes] * old_scale
        if last:
            mixed[:, lanes] = (weighted / total).astype(jnp.bfloat16)
        else:
            new[0][:, lanes] = weighted
            new[1][:, lanes] = total
            new[2][:, lanes] = best
    if last:
        result = ending[0][...].astype(jnp.float32) + jnp.dot(
            mixed[...], ending[1][...], preferred_element_type=jnp.float32
        )
        new[0][...] = result.astype(jnp.bfloat16)


def attend(queries, keyval, parts, ending, name):
    tokens, channels = queries.shape
    last = ending is not None
    part = jax.ShapeDtypeStruct((tokens, channels), jnp.float32)
    whole = jax.ShapeDtypeStruct((tokens, channels), jnp.bfloat16)
    args = [queries, keyval, *(array for each in parts for array in each), *(ending or ())]
    return pl.pallas_call(
        functools.partial(attend_kernel, len(parts), last),
        out_shape=whole if last else (part,) * 3,
        in_specs=[IN_VMEM] * len(args),
        out_specs=IN_VMEM if last else (IN_VMEM,) * 3,
        scratch_shapes=[
            pltpu.VMEM((tokens, channels), jnp.bfloat16),
            pltpu.VMEM((3, tokens, channels) if parts else (3, 8, PAIR), jnp.float32),
        ],
        compiler_params=pltpu.CompilerParams(vmem_limit_bytes=VMEM_BYTES),
        cost_estimate=QUICK,
        name=name,
    )(*args)


def from_edges(top, bottom):
    count = lax.axis_size("band")
    forward = [(i, i + 1) for i in range(count - 1)]
    backward = [(target, source) for source, target in forward]
    return lax.ppermute(bottom, "band", forward), lax.ppermute(top, "band", backward)


def permute(value, pairs):
    bands = lax.axis_size("band")
    flat = [(source[0] * bands + source[1], target[0] * bands + target[1]) for source, target in pairs]
    return lax.ppermute(value, ("frame", "band"), flat)


def ordered(value, *before):
    return lax.optimization_barrier((value, *before))[0]


def step_across(own, is_source, before=()):
    pairs = [((0, b), (1, b)) for b in range(lax.axis_size("band")) if b % 2]
    if lax.axis_size("frame") == 1:
        return own
    return jnp.where(is_source, own, ordered(permute(own, pairs), *before))


def cast(roots, before=()):
    frames, bands = lax.axis_size("frame"), lax.axis_size("band")
    places = frames // 2
    held, reach = list(roots), places
    while reach > 1:
        reach //= 2
        pairs = [
            ((2 * i + b % 2, b), (2 * (i + reach) + b % 2, b))
            for i in range(0, places, 2 * reach)
            for b in range(bands)
        ]
        arrived = [permute(each, pairs) for each in held]
        if before:
            arrived[0] = ordered(arrived[0], *before)
        held = [have + new for have, new in zip(held, arrived)]
        before = ()
    return held


def exchange(held):
    frames, bands = lax.axis_size("frame"), lax.axis_size("band")
    holders = [(f, b) for f in range(frames) for b in range(bands) if f % 2 == b % 2]
    diagonal = permute(held, [((f, b), (f ^ 1, b ^ 2)) for f, b in holders if f != 1])
    beside = permute(held, [((f, b), (f ^ 1, b)) for f, b in holders if f != 1])
    far = permute(
        held,
        [((f, b), (f, b ^ 2)) for f, b in holders] + [((0, b), (0, b ^ 2)) for b in range(bands) if b % 2],
    )
    return beside, diagonal, far


def swap_cores(value):
    frames, bands = lax.axis_size("frame"), lax.axis_size("band")
    return permute(value, [((f, b), (f, b ^ 1)) for f in range(frames) for b in range(bands)])


def own_side(held, parts):
    beside, diagonal, far = parts
    return [held + beside, far + diagonal]


def sees_all(chunks, starts, early, keyval_of, look):
    frames, bands = lax.axis_size("frame"), lax.axis_size("band")
    if frames < 2 or frames & (frames - 1) or bands != 4:
        return [], keyval_of([lax.all_gather(chunk, ("frame", "band"))[b] for chunk in chunks for b in range(bands)])
    held0, held1 = cast(starts, (*early, starts[1]))
    parts0 = exchange(held0)
    parts0 = (parts0[2], parts0[1], parts0[0])
    held1 = ordered(held1, held0)
    parts1 = exchange(held1)
    parts1 = (parts1[2], parts1[0], parts1[1])
    here0 = keyval_of(own_side(held0, [ordered(parts0, held1)[i] for i in (2, 1, 0)]))
    there0 = swap_cores(here0)
    look0 = look(here0)
    here1 = keyval_of(own_side(held1, [ordered(parts1, look0)[i] for i in (1, 2, 0)]))
    there1 = swap_cores(here1)
    look1 = look(ordered(there0, look0, here1))
    look2 = look(ordered(here1, look1))
    return [look0, look1, look2], ordered(there1, look2)


def per_device(latents, conv_weight, conv_bias, w_query, w_keyval, w_out):
    frames, row_count, width, channels = latents.shape
    tokens = row_count * width
    half = row_count // 2
    taps_weight = conv_weight.reshape(3, 3 * channels, channels)
    inner = ((1, half),)
    outer = ((0, 1), (half + 1, row_count - half - 1))
    seam = (half + 1) * width
    layout = (((0, width), (seam, tokens - seam)), ((width, half * width),))
    latents, is_source = lax.optimization_barrier((latents, lax.axis_index("frame") == 0))
    blocks = [latents[frame].reshape(tokens, channels) for frame in range(frames)]
    first, at_hand, top, bottom, *weight_bias = convolve_inner(
        blocks[0], taps_weight, conv_bias, width, inner
    )
    low, high = from_edges(top, bottom)
    begun = step_across(first, is_source, (low, high))
    second = convolve_outer(at_hand, low, high, *weight_bias, width, outer)
    asked = [
        ask((second, first), at_hand, low, high, taps_weight, conv_bias, w_query, width, (outer, inner), layout)
    ]
    for block in blocks[1:]:
        edges = from_edges(block[:width], block[-width:])
        asked.append(ask((), block, *edges, taps_weight, conv_bias, w_query, width, (outer, inner), layout))
    chunks = (first, second)
    starts = (begun, step_across(second, is_source))

    def keyval_of(pieces):
        return project(pieces, w_keyval)

    def look(keyval):
        return tuple(attend(queries, keyval, (), None, "attend") for _, queries in asked)

    looks, keyval = sees_all(chunks, starts, [queries for _, queries in asked], keyval_of, look)
    results = [
        attend(queries, keyval, [each[i] for each in looks], (hidden, w_out), "join")
        for i, (hidden, queries) in enumerate(asked)
    ]
    return jnp.stack(results).reshape(latents.shape)


def solution(mesh):
    return jax.shard_map(
        per_device,
        mesh=mesh,
        in_specs=(P("frame", "band", None, None), P(), P(), P(), P(), P()),
        out_specs=P("frame", "band", None, None),
        check_vma=False,
    )
```
